32 devices in a mesh: elem: 8 (over y, x, core), four: 4 (over z).
Axes of the slice: x: 2, y: 2, z: 4, core: 2. Of those that a mesh axis runs over, the one named last changes fastest.
Arguments:
- adjoint_velocity: float32 [3, 2, 11, 360448], P(None, None, None, ('elem', 'four')), may hold values from -6 to 6
- base_flow: bfloat16 [3, 2, 11, 360448], P(None, None, None, ('elem', 'four')), may hold values from -6 to 6
- column_widths: float32 [128], P('elem'), may hold values from 0.03 to 0.65
- row_heights: float32 [2], replicated, may hold values from 0.06 to 0.18
- base_phase: int32 [1], replicated, may hold values from 0 to 255
Outputs:
- adjoint_next: float32 [3, 2, 11, 360448], P(None, None, None, ('elem', 'four'))
The draws below stay inside these ranges and needn't reach their ends.
All inputs are finite; a program needn't handle non-finite values.
Results may differ from the reference program's by a relative error of at most 0.0003.
Values sent between devices are 32-bit elements; how exact they have to be, the bound alone decides.
A program may use at most 128 MiB of HBM per device.

```python
import math
import jax
import jax.numpy as jnp
import numpy as np
from jax import lax

Q = 11
PLANES = 256
EX_DEV = 16
EY = 2
ITERS = 3
EX = 128
XN = 1408
N_ELEM = 8


def draw_column_widths(key, part):
    position = jnp.arange(EX, dtype=jnp.float32) / max(EX - 1, 1)
    rough = jax.random.uniform(key, (EX,), jnp.float32, 0.75, 1.35)
    return 0.06 * jnp.power(3.0, position) * rough


def block_scale(key, shape, split, low, top_value):
    factor_of = 1.0
    for dim, blocks in split:
        draws = jax.random.uniform(jax.random.fold_in(jax.random.fold_in(key, 6), dim), (blocks,), jnp.float32, low / len(split), top_value / len(split))
        factor_of = factor_of * jnp.repeat(jnp.exp(draws), shape[dim] // blocks).reshape((-1,) + (1,) * (len(shape) - 1 - dim))
    return factor_of


def bell_draw(rng, dims, width, most, cuts=(), kind=jnp.bfloat16):
    factor_of = block_scale(rng, dims, cuts, -0.22, 0.18) if cuts else 1.0
    array = jax.random.normal(rng, dims, jnp.float32) * width * factor_of
    return jnp.minimum(jnp.maximum(array, -most), most).astype(kind)


def setup_inputs(seed: int = 0) -> dict:
    seeds = jax.random.split(jax.random.key(seed), 6)
    adjoint_velocity = bell_draw(seeds[0], (3, EY, Q, N_ELEM * PLANES * EX_DEV * Q), 1.0, 6.0, ((3, 32),), jnp.float32)
    base_flow = bell_draw(seeds[1], (3, EY, Q, XN * PLANES), 1.0, 6.0, ((3, 32),))
    column_widths = draw_column_widths(jax.random.fold_in(seeds[5], 71), 0)
    row_heights = jnp.clip(jnp.exp(jax.random.uniform(seeds[3], (EY,), jnp.float32, math.log(0.06), math.log(0.18))), 0.06, 0.18)
    base_phase = jax.random.randint(seeds[4], (1,), 0, PLANES).astype(jnp.int32)
    return dict(adjoint_velocity=adjoint_velocity, base_flow=base_flow, column_widths=column_widths, row_heights=row_heights, base_phase=base_phase)


NU = 0.005
DT = 0.01
SIGMA = 1.0 / (NU * DT)
HIGHEST = lax.Precision.HIGHEST

def legendre_values(points, node_count):
    table_rows = np.zeros((points.shape[0], node_count))
    table_rows[:, 0] = 1.0
    table_rows[:, 1] = points
    for degree_now in range(2, node_count):
        table_rows[:, degree_now] = ((2 * degree_now - 1) * points * table_rows[:, degree_now - 1] - (degree_now - 1) * table_rows[:, degree_now - 2]) / degree_now
    return table_rows

def gll_tables(node_count):
    degree = node_count - 1
    points = np.cos(np.pi * np.arange(node_count) / degree)
    for newton_step in range(60):
        legendre = legendre_values(points, node_count)
        points = points - (points * legendre[:, degree] - legendre[:, degree - 1]) / (node_count * legendre[:, degree])
    legendre = legendre_values(points, node_count)
    weights = 2.0 / (degree * node_count * legendre[:, degree] ** 2)
    points = points[::-1]
    weights = weights[::-1]
    end_values = legendre[::-1, degree]
    derivative = np.zeros((node_count, node_count))
    for row_index in range(node_count):
        for column in range(node_count):
            if row_index != column:
                derivative[row_index, column] = end_values[row_index] / (end_values[column] * (points[row_index] - points[column]))
    derivative[0, 0] = -degree * node_count / 4.0
    derivative[degree, degree] = degree * node_count / 4.0
    return (jnp.asarray(derivative.astype(np.float32)), jnp.asarray(weights.astype(np.float32)))

def fourier_table(plane_count):
    positions = np.arange(plane_count)
    basis_rows = np.zeros((plane_count, plane_count))
    basis_rows[0] = 1.0 / np.sqrt(plane_count)
    basis_rows[1] = np.cos(np.pi * positions) / np.sqrt(plane_count)
    for wave_index in range(1, plane_count // 2):
        basis_rows[2 * wave_index] = np.sqrt(2.0 / plane_count) * np.cos(2.0 * np.pi * wave_index * positions / plane_count)
        basis_rows[2 * wave_index + 1] = np.sqrt(2.0 / plane_count) * np.sin(2.0 * np.pi * wave_index * positions / plane_count)
    wave_counts = np.arange(plane_count) // 2
    wave_counts[1] = plane_count // 2
    wave_counts[0] = 0
    wavenumbers = 2.0 * np.pi * wave_counts / (plane_count / 64.0)
    rotate = np.zeros((plane_count, plane_count))
    for wave_index in range(1, plane_count // 2):
        rotate[2 * wave_index, 2 * wave_index + 1] = wavenumbers[2 * wave_index]
        rotate[2 * wave_index + 1, 2 * wave_index] = -wavenumbers[2 * wave_index]
    span_slope = basis_rows.T @ rotate @ basis_rows
    return (jnp.asarray(basis_rows.astype(np.float32)), jnp.asarray(wavenumbers.astype(np.float32)), jnp.asarray(span_slope.astype(np.float32)))

def slope_width(values, widths, derivative):
    node_count = derivative.shape[0]
    shaped = values.reshape(values.shape[:-1] + (widths.shape[0], node_count))
    turned = jnp.einsum('km,...xm->...xk', derivative, shaped, precision=HIGHEST)
    return (turned * (2.0 / widths)[:, None]).reshape(values.shape)

def slope_height(values, heights, derivative):
    turned = jnp.einsum('km,...ympx->...ykpx', derivative, values, precision=HIGHEST)
    return turned * (2.0 / heights).reshape(-1, 1, 1, 1)

def slope_span(values, span_slope):
    return jnp.einsum('zw,...wx->...zx', span_slope, values, precision=HIGHEST)

def gradients(values, widths, heights, derivative, span_slope):
    return (slope_width(values, widths, derivative), slope_height(values, heights, derivative), slope_span(values, span_slope))

def advect(line_values, slopes, base_now, base_slopes):
    pieces = []
    for component in range(3):
        summed = base_now[0] * slopes[0][component] + base_now[1] * slopes[1][component] + base_now[2] * slopes[2][component]
        summed = summed - (line_values[0] * base_slopes[component][0] + line_values[1] * base_slopes[component][1] + line_values[2] * base_slopes[component][2])
        pieces.append(summed)
    return jnp.stack(pieces)

def to_lines(basis_rows, coeffs):
    return jnp.einsum('jz,...jx->...zx', basis_rows, coeffs, precision=HIGHEST)

def to_coeffs(basis_rows, line_values):
    return jnp.einsum('jz,...zx->...jx', basis_rows, line_values, precision=HIGHEST)

def mass_factor(widths, heights, weights):
    node_count = weights.shape[0]
    width_b = widths.reshape(1, 1, 1, -1, 1)
    height_b = heights.reshape(-1, 1, 1, 1, 1)
    return width_b * height_b * 0.25 * weights.reshape(1, node_count, 1, 1, 1) * weights.reshape(1, 1, 1, 1, node_count)

def local_operator(values, widths, heights, weights, derivative, wave_sq):
    node_count = derivative.shape[0]
    column_count = widths.shape[0]
    shaped = values.reshape(values.shape[:-1] + (column_count, node_count))
    height_b = heights.reshape(-1, 1, 1, 1, 1)
    width_b = widths.reshape(1, 1, 1, column_count, 1)
    weight_y = weights.reshape(1, node_count, 1, 1, 1)
    weight_x = weights.reshape(1, 1, 1, 1, node_count)
    along_x = jnp.einsum('km,...xm->...xk', derivative, shaped, precision=HIGHEST) * weight_x
    back_x = jnp.einsum('km,...xk->...xm', derivative, along_x, precision=HIGHEST)
    along_y = jnp.einsum('km,...ympxq->...ykpxq', derivative, shaped, precision=HIGHEST) * weight_y
    back_y = jnp.einsum('km,...ykpxq->...ympxq', derivative, along_y, precision=HIGHEST)
    wave_b = wave_sq.reshape(1, 1, -1, 1, 1)
    summed = height_b / width_b * weight_y * back_x + width_b / height_b * weight_x * back_y
    summed = summed + (wave_b + SIGMA) * (width_b * height_b * 0.25) * weight_y * weight_x * shaped
    return summed.reshape(values.shape)

def assemble(values, left_ghost, right_ghost, node_count):
    shaped = values.reshape(values.shape[:-1] + (values.shape[-1] // node_count, node_count))
    first_col = shaped[..., 0]
    last_col = shaped[..., node_count - 1]
    from_left = jnp.concatenate([left_ghost[..., None], last_col[..., :-1]], axis=-1)
    from_right = jnp.concatenate([first_col[..., 1:], right_ghost[..., None]], axis=-1)
    shaped = jnp.concatenate([(first_col + from_left)[..., None], shaped[..., 1:node_count - 1], (last_col + from_right)[..., None]], axis=-1)
    joined = shaped.reshape(values.shape)
    first_row = joined[..., :, 0, :, :]
    last_row = joined[..., :, node_count - 1, :, :]
    shared = last_row[..., :-1, :, :] + first_row[..., 1:, :, :]
    new_first = jnp.concatenate([first_row[..., :1, :, :], shared], axis=-3)
    new_last = jnp.concatenate([shared, last_row[..., -1:, :, :]], axis=-3)
    return jnp.concatenate([new_first[..., :, None, :, :], joined[..., :, 1:node_count - 1, :, :], new_last[..., :, None, :, :]], axis=-3)

def inner_product(left, right, weight):
    return lax.optimization_barrier(jnp.sum(left * right * weight, axis=(-4, -3, -1), keepdims=True))

def reference(adjoint_velocity, base_flow, column_widths, row_heights, base_phase):
    part_nodes = EX_DEV * Q
    packed = adjoint_velocity.reshape(3, EY, Q, N_ELEM, PLANES, part_nodes)
    adjoint_full = jnp.transpose(packed, (0, 1, 2, 4, 3, 5)).reshape(3, EY, Q, PLANES, XN)
    base_full = jnp.transpose(base_flow.reshape(3, EY, Q, XN, PLANES), (0, 1, 2, 4, 3))
    basis_rows, wavenumbers, span_slope = fourier_table(PLANES)
    derivative, weights = gll_tables(Q)
    rolled = jnp.roll(base_full, base_phase[0], axis=3)
    zero_index = jnp.zeros((), jnp.int32)

    def column_step(column_index, accumulated):
        offset = (column_index * Q).astype(jnp.int32)
        coeffs = lax.dynamic_slice_in_dim(adjoint_full, offset, Q, axis=4)
        base_now = lax.dynamic_slice_in_dim(rolled, offset, Q, axis=4).astype(jnp.float32)
        width_here = lax.dynamic_slice_in_dim(column_widths, column_index.astype(jnp.int32), 1)
        line_values = to_lines(basis_rows, coeffs)
        slopes = gradients(line_values, width_here, row_heights, derivative, span_slope)
        base_slopes = gradients(base_now, width_here, row_heights, derivative, span_slope)
        returned = to_coeffs(basis_rows, advect(line_values, slopes, base_now, base_slopes))
        source = SIGMA * coeffs + returned / NU
        shaped = source.reshape(source.shape[:-1] + (1, Q))
        local_part = (mass_factor(width_here, row_heights, weights) * shaped).reshape(source.shape)
        return lax.dynamic_update_slice_in_dim(accumulated, local_part, offset, axis=4)
    local_side = lax.fori_loop(0, EX, column_step, jnp.zeros(adjoint_full.shape, jnp.float32))
    ghost = jnp.zeros(local_side.shape[:-1], jnp.float32)
    right_full = assemble(local_side, ghost, ghost, Q)
    node_x = jnp.arange(EX * Q, dtype=jnp.int32)
    place_x = node_x % Q
    column_x = node_x // Q
    shared_x = (place_x == 0) & (column_x > 0) | (place_x == Q - 1) & (column_x < EX - 1)
    node_y = jnp.arange(EY * Q, dtype=jnp.int32)
    place_y = node_y % Q
    row_y = node_y // Q
    shared_y = (place_y == 0) & (row_y > 0) | (place_y == Q - 1) & (row_y < EY - 1)
    mult_x = 1.0 + shared_x.astype(jnp.float32)
    mult_y = 1.0 + shared_y.astype(jnp.float32)
    weight = (1.0 / (mult_y[:, None] * mult_x[None, :])).reshape(EY, Q, 1, EX * Q)
    blocks = PLANES // 16
    wave_sq_all = wavenumbers * wavenumbers
    ghost_block = jnp.zeros((EY, Q, 16), jnp.float32)

    def helmholtz(values, wave_sq):
        return assemble(local_operator(values, column_widths, row_heights, weights, derivative, wave_sq), ghost_block, ghost_block, Q)

    def solve_block(job_index):
        component = (job_index // blocks).astype(jnp.int32)
        block_index = (job_index % blocks).astype(jnp.int32)
        right_side = lax.dynamic_slice(right_full, (component, zero_index, zero_index, block_index * 16, zero_index), (1, EY, Q, 16, EX * Q))[0]
        wave_sq = lax.dynamic_slice_in_dim(wave_sq_all, block_index * 16, 16)
        solution = jnp.zeros_like(right_side)
        residual = right_side
        direction = right_side
        norm_now = inner_product(residual, residual, weight)
        for iteration in range(ITERS):
            image_vec = helmholtz(direction, wave_sq)
            step_size = norm_now / inner_product(direction, image_vec, weight)
            solution = solution + step_size * direction
            residual = residual - step_size * image_vec
            norm_next = inner_product(residual, residual, weight)
            direction = residual + norm_next / norm_now * direction
            norm_now = norm_next
        return solution
    solved = lax.map(solve_block, jnp.arange(3 * blocks, dtype=jnp.int32))
    solved = solved.reshape(3, blocks, EY, Q, 16, EX * Q)
    solved = jnp.transpose(solved, (0, 2, 3, 1, 4, 5)).reshape(3, EY, Q, PLANES, N_ELEM, part_nodes)
    return jnp.transpose(solved, (0, 1, 2, 4, 3, 5)).reshape(3, EY, Q, N_ELEM * PLANES * part_nodes)
```

```python
import jax
import jax.numpy as jnp
import numpy as np
from jax import lax
from jax.experimental import pallas as pl
from jax.experimental.pallas import tpu as pltpu
from jax.sharding import PartitionSpec as P

ITERS = 3


NU = 0.005
DT = 0.01
SIGMA = 1.0 / (NU * DT)
HIGHEST = lax.Precision.HIGHEST


def padded(x, sides, width):
    for axis, dim in sides:
        count, length = (lax.axis_size(axis), x.shape[dim])
        up = [(i, (i + 1) % count) for i in range(count - 1)]
        down = [(j, i) for i, j in up]
        last = lax.slice_in_dim(x, length - width, length, axis=dim)
        first = lax.slice_in_dim(x, 0, width, axis=dim)
        before = lax.ppermute(last, axis, up)
        after = lax.ppermute(first, axis, down)
        x = jnp.concatenate([before, x, after], axis=dim)
    return x


def legendre_values(points, node_count):
    table_rows = np.zeros((points.shape[0], node_count))
    table_rows[:, 0] = 1.0
    table_rows[:, 1] = points
    for degree_now in range(2, node_count):
        table_rows[:, degree_now] = (
            (2 * degree_now - 1) * points * table_rows[:, degree_now - 1]
            - (degree_now - 1) * table_rows[:, degree_now - 2]
        ) / degree_now
    return table_rows


def gll_tables(node_count):
    degree = node_count - 1
    points = np.cos(np.pi * np.arange(node_count) / degree)
    for newton_step in range(60):
        legendre = legendre_values(points, node_count)
        points = points - (points * legendre[:, degree] - legendre[:, degree - 1]) / (
            node_count * legendre[:, degree]
        )
    legendre = legendre_values(points, node_count)
    weights = 2.0 / (degree * node_count * legendre[:, degree] ** 2)
    points = points[::-1]
    weights = weights[::-1]
    end_values = legendre[::-1, degree]
    derivative = np.zeros((node_count, node_count))
    for row_index in range(node_count):
        for column in range(node_count):
            if row_index != column:
                derivative[row_index, column] = end_values[row_index] / (
                    end_values[column] * (points[row_index] - points[column])
                )
    derivative[0, 0] = -degree * node_count / 4.0
    derivative[degree, degree] = degree * node_count / 4.0
    return (jnp.asarray(derivative.astype(np.float32)), jnp.asarray(weights.astype(np.float32)))


def fourier_table(plane_count):
    positions = np.arange(plane_count)
    basis_rows = np.zeros((plane_count, plane_count))
    basis_rows[0] = 1.0 / np.sqrt(plane_count)
    basis_rows[1] = np.cos(np.pi * positions) / np.sqrt(plane_count)
    for wave_index in range(1, plane_count // 2):
        basis_rows[2 * wave_index] = np.sqrt(2.0 / plane_count) * np.cos(
            2.0 * np.pi * wave_index * positions / plane_count
        )
        basis_rows[2 * wave_index + 1] = np.sqrt(2.0 / plane_count) * np.sin(
            2.0 * np.pi * wave_index * positions / plane_count
        )
    wave_counts = np.arange(plane_count) // 2
    wave_counts[1] = plane_count // 2
    wave_counts[0] = 0
    wavenumbers = 2.0 * np.pi * wave_counts / (plane_count / 64.0)
    rotate = np.zeros((plane_count, plane_count))
    for wave_index in range(1, plane_count // 2):
        rotate[2 * wave_index, 2 * wave_index + 1] = wavenumbers[2 * wave_index]
        rotate[2 * wave_index + 1, 2 * wave_index] = -wavenumbers[2 * wave_index]
    span_slope = basis_rows.T @ rotate @ basis_rows
    return (
        jnp.asarray(basis_rows.astype(np.float32)),
        jnp.asarray(wavenumbers.astype(np.float32)),
        jnp.asarray(span_slope.astype(np.float32)),
    )


def slope_height(values, heights, derivative):
    turned = jnp.einsum("km,...ympx->...ykpx", derivative, values, precision=HIGHEST)
    return turned * (2.0 / heights).reshape(-1, 1, 1, 1)


def line_slope_width(values, widths, derivative):
    node_count = derivative.shape[0]
    shaped = values.reshape(values.shape[:-2] + (widths.shape[0], node_count, values.shape[-1]))
    turned = jnp.einsum("km,...cmz->...ckz", derivative, shaped, precision=HIGHEST)
    return (turned * (2.0 / widths)[:, None, None]).reshape(values.shape)


def line_slope_span(values, span_slope):
    return jnp.einsum("zw,...w->...z", span_slope, values, precision=HIGHEST)


def line_gradients(values, widths, heights, derivative, span_slope):
    return (
        line_slope_width(values, widths, derivative),
        slope_height(values, heights, derivative),
        line_slope_span(values, span_slope),
    )


def advect(line_values, slopes, base_now, base_slopes):
    pieces = []
    for component in range(3):
        summed = (
            base_now[0] * slopes[0][component]
            + base_now[1] * slopes[1][component]
            + base_now[2] * slopes[2][component]
        )
        summed = summed - (
            line_values[0] * base_slopes[component][0]
            + line_values[1] * base_slopes[component][1]
            + line_values[2] * base_slopes[component][2]
        )
        pieces.append(summed)
    return jnp.stack(pieces)


def assemble_rows(joined, node_count):
    first_row = joined[..., :, 0, :, :]
    last_row = joined[..., :, node_count - 1, :, :]
    shared = last_row[..., :-1, :, :] + first_row[..., 1:, :, :]
    new_first = jnp.concatenate([first_row[..., :1, :, :], shared], axis=-3)
    new_last = jnp.concatenate([shared, last_row[..., -1:, :, :]], axis=-3)
    return jnp.concatenate(
        [
            new_first[..., :, None, :, :],
            joined[..., :, 1 : node_count - 1, :, :],
            new_last[..., :, None, :, :],
        ],
        axis=-3,
    )


def edge_assemble(values, is_first, is_last, node_count):
    extended = padded(values, (("elem", 4),), 1)
    following = extended[..., 2:]
    preceding = extended[..., :-2]
    joined = values + jnp.where(is_last, following, 0.0) + jnp.where(is_first, preceding, 0.0)
    return assemble_rows(joined, node_count)


def inner_product(left, right, weight):
    return jnp.sum(left * right * weight, axis=(-4, -3, -1), keepdims=True)


def paired_products(residual, image_vec, weight):
    return lax.psum(
        (inner_product(residual, residual, weight), inner_product(residual, image_vec, weight)),
        "elem",
    )


def local_general(adjoint_velocity, base_flow, column_widths, row_heights, base_phase):
    node_count = adjoint_velocity.shape[2]
    row_count = adjoint_velocity.shape[1]
    columns_here = column_widths.shape[0]
    part_nodes = columns_here * node_count
    planes_local = adjoint_velocity.shape[3] // part_nodes
    adjoint_local = adjoint_velocity.reshape(3, row_count, node_count, planes_local, part_nodes)
    plane_parts = lax.axis_size("four")
    plane_total = planes_local * plane_parts
    columns_line = columns_here // plane_parts
    line_nodes = columns_line * node_count
    base_local = base_flow.reshape(3, row_count, node_count, line_nodes, plane_total)
    basis_rows, wavenumbers, span_slope = fourier_table(plane_total)
    derivative, weights = gll_tables(node_count)
    wave_local = lax.dynamic_slice_in_dim(
        wavenumbers, lax.axis_index("four") * planes_local, planes_local
    )
    line_widths = lax.dynamic_slice_in_dim(
        column_widths, lax.axis_index("four") * columns_line, columns_line
    )
    node_widths = jnp.repeat(column_widths, node_count)
    node_weights = jnp.tile(weights, columns_here)
    eye_cols = jnp.eye(columns_here, dtype=jnp.float32)
    block_turn = jnp.kron(eye_cols, derivative.T)
    block_back = jnp.kron(eye_cols, derivative)
    base_now = jnp.roll(base_local.astype(jnp.float32), base_phase[0], axis=4)
    base_slopes = line_gradients(base_now, line_widths, row_heights, derivative, span_slope)
    sending = jnp.transpose(adjoint_local, (0, 1, 2, 4, 3))
    arrived = lax.all_to_all(sending, "four", split_axis=3, concat_axis=4, tiled=True)
    line_values = jnp.einsum("jz,...xj->...xz", basis_rows, arrived, precision=HIGHEST)
    slopes = line_gradients(line_values, line_widths, row_heights, derivative, span_slope)
    advection = advect(line_values, slopes, base_now, base_slopes)
    advection_hat = jnp.einsum("jz,...xz->...xj", basis_rows, advection, precision=HIGHEST)
    returned = lax.all_to_all(advection_hat, "four", split_axis=4, concat_axis=3, tiled=True)
    returned = jnp.transpose(returned, (0, 1, 2, 4, 3))
    node_x = jnp.arange(part_nodes, dtype=jnp.int32)
    place_x = node_x % node_count
    is_first = place_x == 0
    is_last = place_x == node_count - 1
    height_b = row_heights.reshape(-1, 1, 1, 1)
    weight_y = weights.reshape(-1, 1, 1)
    source = SIGMA * adjoint_local + returned / NU
    local_side = node_widths * height_b * 0.25 * weight_y * node_weights * source
    right_side = edge_assemble(local_side, is_first, is_last, node_count)
    column_x = lax.axis_index("elem") * columns_here + node_x // node_count
    last_column = columns_here * lax.axis_size("elem") - 1
    shared_x = is_first & (column_x > 0) | is_last & (column_x < last_column)
    node_y = jnp.arange(row_count * node_count, dtype=jnp.int32)
    place_y = node_y % node_count
    row_y = node_y // node_count
    shared_y = (place_y == 0) & (row_y > 0) | (place_y == node_count - 1) & (row_y < row_count - 1)
    mult_x = 1.0 + shared_x.astype(jnp.float32)
    mult_y = 1.0 + shared_y.astype(jnp.float32)
    weight = (1.0 / (mult_y[:, None] * mult_x[None, :])).reshape(
        row_count, node_count, 1, part_nodes
    )
    wave_b = (wave_local * wave_local).reshape(-1, 1)

    def helmholtz(values):
        along_x = jnp.einsum("...n,nm->...m", values, block_turn, precision=HIGHEST) * node_weights
        back_x = jnp.einsum("...n,nm->...m", along_x, block_back, precision=HIGHEST)
        along_y = (
            jnp.einsum("km,...ympx->...ykpx", derivative, values, precision=HIGHEST) * weight_y
        )
        back_y = jnp.einsum("km,...ykpx->...ympx", derivative, along_y, precision=HIGHEST)
        summed = (
            height_b / node_widths * weight_y * back_x
            + node_widths / height_b * node_weights * back_y
        )
        summed = (
            summed
            + (wave_b + SIGMA) * (node_widths * height_b * 0.25) * weight_y * node_weights * values
        )
        return edge_assemble(summed, is_first, is_last, node_count)

    solution = jnp.zeros_like(right_side)
    residual = right_side
    image_vec = helmholtz(residual)
    norm_now, product = paired_products(residual, image_vec, weight)
    step_size = norm_now / product
    direction = residual
    along = image_vec
    for iteration in range(ITERS):
        solution = solution + step_size * direction
        residual = residual - step_size * along
        if iteration + 1 < ITERS:
            image_vec = helmholtz(residual)
            norm_next, product = paired_products(residual, image_vec, weight)
            growth = norm_next / norm_now
            step_size = norm_next / (product - growth * norm_next / step_size)
            direction = residual + growth * direction
            along = image_vec + growth * along
            norm_now = norm_next
    return solution.reshape(3, row_count, node_count, planes_local * part_nodes)


MESH = pl.DeviceIdType.MESH
NODES = 121
PAD = 122
TILES = 61
LANES = 128


def gll_numbers(node_count):
    degree = node_count - 1
    points = np.cos(np.pi * np.arange(node_count) / degree)
    for newton_step in range(60):
        legendre = legendre_values(points, node_count)
        points = points - (points * legendre[:, degree] - legendre[:, degree - 1]) / (
            node_count * legendre[:, degree]
        )
    legendre = legendre_values(points, node_count)
    weights = (2.0 / (degree * node_count * legendre[:, degree] ** 2))[::-1]
    points = points[::-1]
    end_values = legendre[::-1, degree]
    derivative = np.zeros((node_count, node_count))
    for row_index in range(node_count):
        for column in range(node_count):
            if row_index != column:
                derivative[row_index, column] = end_values[row_index] / (
                    end_values[column] * (points[row_index] - points[column])
                )
    derivative[0, 0] = -degree * node_count / 4.0
    derivative[degree, degree] = degree * node_count / 4.0
    derivative = derivative.astype(np.float32).astype(np.float64)
    weights = weights.astype(np.float32).astype(np.float64)
    return derivative, weights


def span_numbers(plane_count):
    positions = np.arange(plane_count)
    basis_rows = np.zeros((plane_count, plane_count))
    basis_rows[0] = 1.0 / np.sqrt(plane_count)
    basis_rows[1] = np.cos(np.pi * positions) / np.sqrt(plane_count)
    for wave_index in range(1, plane_count // 2):
        basis_rows[2 * wave_index] = np.sqrt(2.0 / plane_count) * np.cos(
            2.0 * np.pi * wave_index * positions / plane_count
        )
        basis_rows[2 * wave_index + 1] = np.sqrt(2.0 / plane_count) * np.sin(
            2.0 * np.pi * wave_index * positions / plane_count
        )
    wave_counts = np.arange(plane_count) // 2
    wave_counts[1] = plane_count // 2
    wave_counts[0] = 0
    wavenumbers = 2.0 * np.pi * wave_counts / (plane_count / 64.0)
    rotate = np.zeros((plane_count, plane_count))
    for wave_index in range(1, plane_count // 2):
        rotate[2 * wave_index, 2 * wave_index + 1] = wavenumbers[2 * wave_index]
        rotate[2 * wave_index + 1, 2 * wave_index] = -wavenumbers[2 * wave_index]
    return basis_rows, basis_rows.T @ rotate @ basis_rows


def two_parts(table):
    table = table.astype(np.float32)
    high = table.astype(jnp.bfloat16)
    low = (table - high.astype(np.float32)).astype(jnp.bfloat16)
    return high, low


def split_values(values):
    high = values.astype(jnp.bfloat16)
    low = (values - high.astype(jnp.float32)).astype(jnp.bfloat16)
    return high, low


def dot(left, right):
    return jnp.dot(left, right, preferred_element_type=jnp.float32)


def dot_three(values, high, low):
    vh, vl = split_values(values)
    return dot(vh, high) + (dot(vl, high) + dot(vh, low))


def times(matrix, values, sign):
    n = len(values)
    half = n // 2
    even = [values[m] + values[n - 1 - m] for m in range(half)]
    odd = [values[m] - values[n - 1 - m] for m in range(half)]
    out = [None] * n
    for k in range(half + 1):
        s = None
        d = None
        for m in range(half):
            ce = 0.5 * (matrix[k, m] + matrix[k, n - 1 - m])
            co = 0.5 * (matrix[k, m] - matrix[k, n - 1 - m])
            if not (k == half and sign < 0):
                term = float(ce) * even[m]
                s = term if s is None else s + term
            if not (k == half and sign > 0):
                term = float(co) * odd[m]
                d = term if d is None else d + term
        if not (k == half and sign < 0):
            s = s + float(matrix[k, half]) * values[half]
        if k == half:
            out[k] = s if sign > 0 else d
        else:
            out[k] = s + d
            out[n - 1 - k] = s - d if sign > 0 else d - s
    return out


def swap_halves(a, b, low):
    axis = a.ndim - 2
    return (
        jnp.where(low, a, pltpu.roll(b, 4, axis)),
        jnp.where(low, pltpu.roll(a, 4, axis), b),
    )


def chunk_start(step, size, total):
    return jnp.minimum(step * size, total - size)


def section_kernel(
    sizes,
    derivative,
    weights,
    coef_ref,
    base_ref,
    wh_ref,
    wl_ref,
    vh_ref,
    vl_ref,
    dh_ref,
    dl_ref,
    widths_ref,
    heights_ref,
    phase_ref,
    wq_ref,
    out_ref,
    send1,
    recv1,
    send2,
    recv2,
    base_now,
    base_slope,
    lines,
    line_z,
    acc,
    res,
    image,
    direction,
    along,
    edges,
    ghosts,
    sums,
    sums_in,
    send1_sem,
    recv1_sem,
    send2_sem,
    recv2_sem,
    local_sem,
    edge_send_sem,
    edge_recv_sem,
    sum_send_sem,
    sum_recv_sem,
):
    n_four, n_elem = sizes
    q = 11
    elem = lax.axis_index("elem")
    four = lax.axis_index("four")
    stiff = derivative.T @ (weights[:, None] * derivative)

    barrier = pltpu.get_barrier_semaphore()
    for k in range(1, n_four):
        pl.semaphore_signal(
            barrier, inc=1, device_id=(elem, lax.rem(four + k, n_four)), device_id_type=MESH
        )
    for k in range(1, n_elem):
        pl.semaphore_signal(
            barrier, inc=1, device_id=(lax.rem(elem + k, n_elem), four), device_id_type=MESH
        )

    low3 = lax.broadcasted_iota(jnp.int32, (1, 8, LANES), 1) < 4
    low3w = lax.broadcasted_iota(jnp.int32, (1, 8, 256), 1) < 4

    def pack(c):
        def body(step, carry):
            t = chunk_start(step, 8, TILES)
            for tile in range(2):
                a = coef_ref[c, pl.ds(t, 8), pl.ds(8 * tile, 8), :]
                b = coef_ref[c, pl.ds(t + TILES, 8), pl.ds(8 * tile, 8), :]
                first, second = swap_halves(a, b, low3)
                send1[2 * tile, c, pl.ds(t, 8)] = first
                send1[2 * tile + 1, c, pl.ds(t, 8)] = second
            return carry

        lax.fori_loop(0, 8, body, 0)

    def exchange(source, target, send_sem, recv_sem, c):
        return [
            pltpu.make_async_remote_copy(
                src_ref=source.at[lax.rem(four + k, n_four), c],
                dst_ref=target.at[four, c],
                send_sem=send_sem.at[c, k],
                recv_sem=recv_sem.at[c, k],
                device_id=(elem, lax.rem(four + k, n_four)),
                device_id_type=MESH,
            )
            for k in range(1, n_four)
        ]

    def own(source, target, c, which):
        return pltpu.make_async_copy(source.at[four, c], target.at[four, c], local_sem.at[which, c])

    copies1 = [exchange(send1, recv1, send1_sem, recv1_sem, c) for c in range(3)]
    own1 = [own(send1, recv1, c, 0) for c in range(3)]
    copies2 = [exchange(send2, recv2, send2_sem, recv2_sem, c) for c in range(3)]
    own2 = [own(send2, recv2, c, 1) for c in range(3)]

    pack(0)
    pl.semaphore_wait(barrier, n_four - 1 + n_elem - 1)
    for copy in copies1[0]:
        copy.start()
    own1[0].start()
    for c in (1, 2):
        pack(c)
        for copy in copies1[c]:
            copy.start()
        own1[c].start()

    row_w = lax.broadcasted_iota(jnp.int32, (8, LANES), 0)
    first_column = four * 4
    hx = jnp.zeros((8, LANES), jnp.float32)
    hy = jnp.zeros((8, LANES), jnp.float32)
    for i in range(8):
        hx = jnp.where(row_w == i, widths_ref[first_column + i % 4], hx)
        hy = jnp.where(row_w == i, heights_ref[i // 4], hy)
    gx = 2.0 / hx
    gy = 2.0 / hy

    phase = phase_ref[0]
    shift_row = lax.broadcasted_iota(jnp.int32, (256, 256), 0)
    shift_col = lax.broadcasted_iota(jnp.int32, (256, 256), 1)
    moved = jnp.where(shift_row + phase >= 256, shift_row + phase - 256, shift_row + phase)
    shift = jnp.where(moved == shift_col, 1.0, 0.0).astype(jnp.bfloat16)

    for c in range(3):

        def roll_body(step, carry, c=c):
            n = step * 11
            rows = base_ref[c, pl.ds(n, 11)].reshape(88, 256).astype(jnp.bfloat16)
            now = dot(rows, shift)
            base_now[c, pl.ds(n, 11)] = now.reshape(11, 8, 256)
            now_b = now.astype(jnp.bfloat16)
            slope = dot(now_b, dh_ref[...]) + dot(now_b, dl_ref[...])
            base_slope[c, 2, pl.ds(n, 11)] = slope.reshape(11, 8, 256)
            return carry

        lax.fori_loop(0, 11, roll_body, 0)

        def slope_body(step, carry, c=c):
            for h in range(2):
                part = pl.ds(LANES * h, LANES)
                turned = times(
                    derivative, [base_now[c, step * 11 + m, :, part] for m in range(q)], -1
                )
                for k in range(q):
                    base_slope[c, 0, step * 11 + k, :, part] = gx * turned[k]
                turned = times(
                    derivative, [base_now[c, m * 11 + step, :, part] for m in range(q)], -1
                )
                for k in range(q):
                    base_slope[c, 1, k * 11 + step, :, part] = gy * turned[k]
            return carry

        lax.fori_loop(0, 11, slope_body, 0)

    for c in range(3):
        acc[c, NODES] = jnp.zeros((8, 256), jnp.float32)
    edges[...] = jnp.zeros(edges.shape, jnp.float32)
    sums[...] = jnp.zeros(sums.shape, jnp.float32)

    for c in range(3):
        for copy in copies1[c]:
            copy.wait_recv()
        own1[c].wait()

        def line_body(step, carry, c=c):
            t = chunk_start(step, 8, TILES)
            out = None
            for s in range(n_four):
                rows = recv1[s, c, pl.ds(t, 8)].reshape(64, LANES)
                part = dot_three(
                    rows, wh_ref[pl.ds(s * LANES, LANES), :], wl_ref[pl.ds(s * LANES, LANES), :]
                )
                out = part if out is None else out + part
            e0 = out[:, :256].reshape(8, 8, 256)
            e1 = out[:, 256:].reshape(8, 8, 256)
            a, b = swap_halves(e0, e1, low3w)
            lines[pl.ds(t, 8)] = a
            lines[pl.ds(t + TILES, 8)] = b
            return carry

        lax.fori_loop(0, 8, line_body, 0)

        def span_body(step, carry):
            n = step * 11
            rows = lines[pl.ds(n, 11)].reshape(88, 256)
            line_z[pl.ds(n, 11)] = dot_three(rows, dh_ref[...], dl_ref[...]).reshape(11, 8, 256)
            return carry

        lax.fori_loop(0, 11, span_body, 0)

        def add_x(step, carry, c=c):
            for h in range(2):
                part = pl.ds(LANES * h, LANES)
                values = [lines[step * 11 + m, :, part] for m in range(q)]
                turned = times(derivative, values, -1)
                for k in range(q):
                    n = step * 11 + k
                    gain = base_now[0, n, :, part] * (gx * turned[k])
                    gain = gain + base_now[2, n, :, part] * line_z[n, :, part]
                    for e in range(3):
                        change = -values[k] * base_slope[c, e, n, :, part]
                        if e == c:
                            change = change + gain
                        if c > 0:
                            change = change + acc[e, n, :, part]
                        acc[e, n, :, part] = change
            return carry

        lax.fori_loop(0, 11, add_x, 0)

        def add_y(step, carry, c=c):
            for h in range(2):
                part = pl.ds(LANES * h, LANES)
                values = [lines[m * 11 + step, :, part] for m in range(q)]
                turned = times(derivative, values, -1)
                for k in range(q):
                    n = k * 11 + step
                    acc[c, n, :, part] += base_now[1, n, :, part] * (gy * turned[k])
            return carry

        lax.fori_loop(0, 11, add_y, 0)

    for c in range(3):

        def back_body(step, carry, c=c):
            t = chunk_start(step, 8, TILES)
            a = acc[c, pl.ds(t, 8)]
            b = acc[c, pl.ds(t + TILES, 8)]
            e0, e1 = swap_halves(a, b, low3w)
            e0 = e0.reshape(64, 256)
            e1 = e1.reshape(64, 256)
            out = dot_three(e0, vh_ref[pl.ds(0, 256), :], vl_ref[pl.ds(0, 256), :])
            out = out + dot_three(e1, vh_ref[pl.ds(256, 256), :], vl_ref[pl.ds(256, 256), :])
            for s in range(n_four):
                send2[s, c, pl.ds(t, 8)] = out[:, LANES * s : LANES * (s + 1)].reshape(8, 8, LANES)
            return carry

        lax.fori_loop(0, 8, back_body, 0)
        for copy in copies2[c]:
            copy.start()
        own2[c].start()

    lane = lax.broadcasted_iota(jnp.int32, (8, LANES), 1)
    row = lax.broadcasted_iota(jnp.int32, (8, LANES), 0)
    lower = lane < 64
    lane_plane = jnp.where(lower, lane, lane - 64) + four * 64
    kappa = lane_plane // 2
    kappa = jnp.where(lane_plane == 1, 32 * n_four, kappa)
    kappa = jnp.where(lane_plane == 0, 0, kappa)
    beta = kappa.astype(jnp.float32) * np.float32(2.0 * np.pi / n_four)
    wave = beta * beta + SIGMA
    hyl = jnp.where(lower, heights_ref[0], heights_ref[1])
    hxl = []
    for tile in range(2):
        h = jnp.zeros((8, LANES), jnp.float32)
        for i in range(8):
            h = jnp.where(row == i, widths_ref[8 * tile + i], h)
        hxl.append(h)
    quarter = [0.25 * h * hyl for h in hxl]
    scale_x = [hyl / h for h in hxl]
    scale_y = [h / hyl for h in hxl]
    one = jnp.ones((8, LANES), jnp.float32)
    half = 0.5 * one
    left_inner = elem > 0
    right_inner = elem < n_elem - 1
    share_first = [jnp.where(jnp.logical_and(row == 0, jnp.logical_not(left_inner)), one, half), half]
    share_last = [half, jnp.where(jnp.logical_and(row == 7, jnp.logical_not(right_inner)), one, half)]
    share_top = jnp.where(lower, one, half)
    share_bottom = jnp.where(lower, half, one)
    right = lax.rem(elem + 1, n_elem)
    left = lax.rem(elem + n_elem - 1, n_elem)

    def edge_copies(c, level):
        return [
            pltpu.make_async_remote_copy(
                src_ref=edges.at[c, level, 0],
                dst_ref=ghosts.at[c, level, 1],
                send_sem=edge_send_sem.at[c, level, 0],
                recv_sem=edge_recv_sem.at[c, level, 1],
                device_id=(left, four),
                device_id_type=MESH,
            ),
            pltpu.make_async_remote_copy(
                src_ref=edges.at[c, level, 1],
                dst_ref=ghosts.at[c, level, 0],
                send_sem=edge_send_sem.at[c, level, 1],
                recv_sem=edge_recv_sem.at[c, level, 0],
                device_id=(right, four),
                device_id_type=MESH,
            ),
        ]

    def edge_start(values, c, level):
        for qy in range(q):
            edges[c, level, 0, pl.ds(qy, 1), :] = values[qy * 11, pl.ds(0, 1), :]
            edges[c, level, 1, pl.ds(qy, 1), :] = values[qy * 11 + 10, pl.ds(15, 1), :]
        copies = edge_copies(c, level)
        for copy in copies:
            copy.start()
        return copies

    left_keep = jnp.where(left_inner, 1.0, 0.0)
    right_keep = jnp.where(right_inner, 1.0, 0.0)

    def assemble_here(values, c, level, copies):
        for copy in copies:
            copy.wait_recv()

        def body(qy, carry):
            n0 = qy * 11
            a0 = values[n0, pl.ds(0, 8), :]
            a1 = values[n0, pl.ds(8, 8), :]
            b0 = values[n0 + 10, pl.ds(0, 8), :]
            b1 = values[n0 + 10, pl.ds(8, 8), :]
            from_left = ghosts[c, level, 0, pl.ds(qy, 1), :] * left_keep
            from_right = ghosts[c, level, 1, pl.ds(qy, 1), :] * right_keep
            rb0 = pltpu.roll(b0, 1, 0)
            rb1 = pltpu.roll(b1, 1, 0)
            ra0 = pltpu.roll(a0, 7, 0)
            ra1 = pltpu.roll(a1, 7, 0)
            values[n0, pl.ds(0, 8), :] = a0 + jnp.where(row == 0, from_left, rb0)
            values[n0, pl.ds(8, 8), :] = a1 + jnp.where(row == 0, rb0, rb1)
            values[n0 + 10, pl.ds(0, 8), :] = b0 + jnp.where(row == 7, ra1, ra0)
            values[n0 + 10, pl.ds(8, 8), :] = b1 + jnp.where(row == 7, from_right, ra1)
            return carry

        lax.fori_loop(0, q, body, 0)
        for qx in range(q):
            for tile in range(2):
                rows = pl.ds(8 * tile, 8)
                top = values[qx, rows, :]
                bottom = values[110 + qx, rows, :]
                values[qx, rows, :] = top + jnp.where(lower, 0.0, pltpu.roll(bottom, 64, 1))
                values[110 + qx, rows, :] = bottom + jnp.where(lower, pltpu.roll(top, 64, 1), 0.0)

    def sum_copies(c, level):
        return [
            pltpu.make_async_remote_copy(
                src_ref=sums.at[c, level],
                dst_ref=sums_in.at[c, level, k],
                send_sem=sum_send_sem.at[c, level, k],
                recv_sem=sum_recv_sem.at[c, level, k],
                device_id=(lax.rem(elem + k, n_elem), four),
                device_id_type=MESH,
            )
            for k in range(1, n_elem)
        ]

    zero = jnp.zeros((8, LANES), jnp.float32)

    def apply(values, target):
        def body_x(qy, carry):
            rr, wy = carry[0], wq_ref[qy]
            share = jnp.where(qy == 0, share_top, jnp.where(qy == q - 1, share_bottom, one))
            for tile in range(2):
                rows = pl.ds(8 * tile, 8)
                v = [values[qy * 11 + m, rows, :] for m in range(q)]
                turned = times(stiff, v, 1)
                ax = scale_x[tile] * wy
                mass = (wave * quarter[tile]) * wy
                inner = None
                for k in range(q):
                    target[qy * 11 + k, rows, :] = ax * turned[k] + (mass * float(weights[k])) * v[k]
                    square = v[k] * v[k]
                    if k == 0:
                        square = square * share_first[tile]
                    if k == q - 1:
                        square = square * share_last[tile]
                    inner = square if inner is None else inner + square
                rr = rr + share * inner
            return (rr,)

        (rr,) = lax.fori_loop(0, q, body_x, (zero,))

        def body_y(qx, carry):
            product, wx = carry[0], wq_ref[qx]
            for tile in range(2):
                rows = pl.ds(8 * tile, 8)
                v = [values[m * 11 + qx, rows, :] for m in range(q)]
                turned = times(stiff, v, 1)
                ay = scale_y[tile] * wx
                for k in range(q):
                    total = target[k * 11 + qx, rows, :] + ay * turned[k]
                    target[k * 11 + qx, rows, :] = total
                    product = product + v[k] * total
            return (product,)

        (product,) = lax.fori_loop(0, q, body_y, (zero,))
        return rr, product

    def fold(values):
        total = jnp.sum(values, axis=0, keepdims=True)
        return total + pltpu.roll(total, 64, 1)

    waiting = []
    for c in range(3):
        for copy in copies2[c]:
            copy.wait_recv()
        own2[c].wait()

        def unpack_body(step, carry, c=c):
            t = chunk_start(step, 8, TILES)
            for tile in range(2):
                rows = pl.ds(8 * tile, 8)
                a, b = swap_halves(
                    recv2[2 * tile, c, pl.ds(t, 8)], recv2[2 * tile + 1, c, pl.ds(t, 8)], low3
                )
                res[pl.ds(t, 8), rows, :] = SIGMA * coef_ref[c, pl.ds(t, 8), rows, :] + a / NU
                res[pl.ds(t + TILES, 8), rows, :] = (
                    SIGMA * coef_ref[c, pl.ds(t + TILES, 8), rows, :] + b / NU
                )
            return carry

        lax.fori_loop(0, 8, unpack_body, 0)

        def mass_body(qy, carry):
            wy = wq_ref[qy]
            for tile in range(2):
                rows = pl.ds(8 * tile, 8)
                area = quarter[tile] * wy
                for k in range(q):
                    res[qy * 11 + k, rows, :] = res[qy * 11 + k, rows, :] * (area * float(weights[k]))
            return carry

        lax.fori_loop(0, q, mass_body, 0)
        copies = edge_start(res, c, 0)
        waiting += copies
        assemble_here(res, c, 0, copies)

        norm_now = None
        step_size = None
        for it in range(ITERS):
            rr, product = apply(res, image)
            sums[c, it, pl.ds(0, 1), :] = fold(rr)
            sums[c, it, pl.ds(1, 1), :] = fold(product)
            sum_list = sum_copies(c, it)
            for copy in sum_list:
                copy.start()
            waiting += sum_list
            if it + 1 < ITERS:
                copies = edge_start(image, c, it + 1)
                waiting += copies
                assemble_here(image, c, it + 1, copies)
            for copy in sum_list:
                copy.wait_recv()
            total = sums[c, it]
            for k in range(1, n_elem):
                total = total + sums_in[c, it, k]
            norm_next = total[0:1, :]
            product = total[1:2, :]
            if it == 0:
                growth = jnp.zeros_like(norm_next)
                step_size = norm_next / product
            else:
                growth = norm_next / norm_now
                step_size = norm_next / (product - growth * norm_next / step_size)
            norm_now = norm_next

            def update(n, carry, it=it, c=c, growth=growth, step_size=step_size):
                for j in range(11):
                    m = n * 11 + j
                    r = res[m]
                    if it == 0:
                        d = r
                        out_ref[c, m] = step_size * d
                    else:
                        d = r + growth * direction[m]
                        out_ref[c, m] = out_ref[c, m] + step_size * d
                    if it + 1 < ITERS:
                        direction[m] = d
                        a = image[m]
                        if it > 0:
                            a = a + growth * along[m]
                        if it + 2 < ITERS:
                            along[m] = a
                        res[m] = r - step_size * a
                return carry

            lax.fori_loop(0, 11, update, 0)

    for group in copies1 + copies2 + [waiting]:
        for copy in group:
            copy.wait_send()


def local_blocks(adjoint_velocity, base_flow, column_widths, row_heights, base_phase):
    n_four, n_elem = lax.axis_size("four"), lax.axis_size("elem")
    derivative, weights = gll_numbers(11)
    basis_rows, span_slope = span_numbers(256)
    forward = np.zeros((n_four, 2, 64, 2, 256))
    for ey in range(2):
        forward[:, ey, :, ey, :] = basis_rows.reshape(n_four, 64, 256)
    forward = forward.reshape(512, 512)
    tables = two_parts(forward) + two_parts(forward.T) + two_parts(span_slope.T)
    coef = adjoint_velocity.reshape(3, 2, 11, 64, 16, 11)
    coef = jnp.transpose(coef, (0, 2, 5, 4, 1, 3)).reshape(3, NODES, 16, LANES)
    coef = jnp.pad(coef, ((0, 0), (0, PAD - NODES), (0, 0), (0, 0)))
    base = base_flow.reshape(3, 2, 11, 4, 11, 256)
    base = jnp.transpose(base, (0, 2, 4, 1, 3, 5)).reshape(3, NODES, 8, 256).astype(jnp.float32)
    vmem = pl.BlockSpec(memory_space=pltpu.VMEM)
    smem = pl.BlockSpec(memory_space=pltpu.SMEM)
    f32 = jnp.float32
    blocks = (n_four, 3, TILES, 8, LANES)
    field = (PAD, 16, LANES)
    dma = pltpu.SemaphoreType.DMA
    out = pl.pallas_call(
        lambda *refs: section_kernel((n_four, n_elem), derivative, weights, *refs),
        out_shape=jax.ShapeDtypeStruct((3, NODES, 16, LANES), f32),
        in_specs=[vmem] * 8 + [smem] * 4,
        out_specs=vmem,
        scratch_shapes=[
            pltpu.VMEM(blocks, f32),
            pltpu.VMEM(blocks, f32),
            pltpu.VMEM(blocks, f32),
            pltpu.VMEM(blocks, f32),
            pltpu.VMEM((3, NODES, 8, 256), f32),
            pltpu.VMEM((3, 3, NODES, 8, 256), f32),
            pltpu.VMEM((PAD, 8, 256), f32),
            pltpu.VMEM((PAD, 8, 256), f32),
            pltpu.VMEM((3, PAD, 8, 256), f32),
            pltpu.VMEM(field, f32),
            pltpu.VMEM(field, f32),
            pltpu.VMEM(field, f32),
            pltpu.VMEM(field, f32),
            pltpu.VMEM((3, ITERS, 2, 16, LANES), f32),
            pltpu.VMEM((3, ITERS, 2, 16, LANES), f32),
            pltpu.VMEM((3, ITERS, 8, LANES), f32),
            pltpu.VMEM((3, ITERS, n_elem, 8, LANES), f32),
            dma((3, n_four)),
            dma((3, n_four)),
            dma((3, n_four)),
            dma((3, n_four)),
            dma((2, 3)),
            dma((3, ITERS, 2)),
            dma((3, ITERS, 2)),
            dma((3, ITERS, n_elem)),
            dma((3, ITERS, n_elem)),
        ],
        compiler_params=pltpu.CompilerParams(
            collective_id=0, has_side_effects=True, vmem_limit_bytes=60 * 1024 * 1024
        ),
    )(coef, base, *tables, column_widths, row_heights, base_phase, weights.astype(np.float32))
    out = out.reshape(3, 11, 11, 16, 2, 64)
    return jnp.transpose(out, (0, 4, 1, 5, 3, 2)).reshape(adjoint_velocity.shape)


def local(adjoint_velocity, base_flow, column_widths, row_heights, base_phase):
    four, elem = lax.axis_size("four"), lax.axis_size("elem")
    known = (
        adjoint_velocity.shape == (3, 2, 11, 64 * 16 * 11)
        and column_widths.shape == (16,)
        and four == 4
        and elem > 2
    )
    chosen = local_blocks if known else local_general
    return chosen(adjoint_velocity, base_flow, column_widths, row_heights, base_phase)


def solution(mesh):
    return jax.shard_map(
        local,
        mesh=mesh,
        in_specs=(
            P(None, None, None, ("elem", "four")),
            P(None, None, None, ("elem", "four")),
            P("elem"),
            P(),
            P(),
        ),
        out_specs=P(None, None, None, ("elem", "four")),
        check_vma=False,
    )
```

```python
import jax
import jax.numpy as jnp
import numpy as np
from jax import lax
from jax.experimental import pallas as pl
from jax.experimental.pallas import tpu as pltpu
from jax.sharding import PartitionSpec as P

ITERS = 3


NU = 0.005
DT = 0.01
SIGMA = 1.0 / (NU * DT)
HIGHEST = lax.Precision.HIGHEST


def padded(x, sides, width):
    for axis, dim in sides:
        count, length = (lax.axis_size(axis), x.shape[dim])
        up = [(i, (i + 1) % count) for i in range(count - 1)]
        down = [(j, i) for i, j in up]
        last = lax.slice_in_dim(x, length - width, length, axis=dim)
        first = lax.slice_in_dim(x, 0, width, axis=dim)
        before = lax.ppermute(last, axis, up)
        after = lax.ppermute(first, axis, down)
        x = jnp.concatenate([before, x, after], axis=dim)
    return x


def legendre_values(points, node_count):
    table_rows = np.zeros((points.shape[0], node_count))
    table_rows[:, 0] = 1.0
    table_rows[:, 1] = points
    for degree_now in range(2, node_count):
        table_rows[:, degree_now] = (
            (2 * degree_now - 1) * points * table_rows[:, degree_now - 1]
            - (degree_now - 1) * table_rows[:, degree_now - 2]
        ) / degree_now
    return table_rows


def gll_tables(node_count):
    degree = node_count - 1
    points = np.cos(np.pi * np.arange(node_count) / degree)
    for newton_step in range(60):
        legendre = legendre_values(points, node_count)
        points = points - (points * legendre[:, degree] - legendre[:, degree - 1]) / (
            node_count * legendre[:, degree]
        )
    legendre = legendre_values(points, node_count)
    weights = 2.0 / (degree * node_count * legendre[:, degree] ** 2)
    points = points[::-1]
    weights = weights[::-1]
    end_values = legendre[::-1, degree]
    derivative = np.zeros((node_count, node_count))
    for row_index in range(node_count):
        for column in range(node_count):
            if row_index != column:
                derivative[row_index, column] = end_values[row_index] / (
                    end_values[column] * (points[row_index] - points[column])
                )
    derivative[0, 0] = -degree * node_count / 4.0
    derivative[degree, degree] = degree * node_count / 4.0
    return (jnp.asarray(derivative.astype(np.float32)), jnp.asarray(weights.astype(np.float32)))


def fourier_table(plane_count):
    positions = np.arange(plane_count)
    basis_rows = np.zeros((plane_count, plane_count))
    basis_rows[0] = 1.0 / np.sqrt(plane_count)
    basis_rows[1] = np.cos(np.pi * positions) / np.sqrt(plane_count)
    for wave_index in range(1, plane_count // 2):
        basis_rows[2 * wave_index] = np.sqrt(2.0 / plane_count) * np.cos(
            2.0 * np.pi * wave_index * positions / plane_count
        )
        basis_rows[2 * wave_index + 1] = np.sqrt(2.0 / plane_count) * np.sin(
            2.0 * np.pi * wave_index * positions / plane_count
        )
    wave_counts = np.arange(plane_count) // 2
    wave_counts[1] = plane_count // 2
    wave_counts[0] = 0
    wavenumbers = 2.0 * np.pi * wave_counts / (plane_count / 64.0)
    rotate = np.zeros((plane_count, plane_count))
    for wave_index in range(1, plane_count // 2):
        rotate[2 * wave_index, 2 * wave_index + 1] = wavenumbers[2 * wave_index]
        rotate[2 * wave_index + 1, 2 * wave_index] = -wavenumbers[2 * wave_index]
    span_slope = basis_rows.T @ rotate @ basis_rows
    return (
        jnp.asarray(basis_rows.astype(np.float32)),
        jnp.asarray(wavenumbers.astype(np.float32)),
        jnp.asarray(span_slope.astype(np.float32)),
    )


def slope_height(values, heights, derivative):
    turned = jnp.einsum("km,...ympx->...ykpx", derivative, values, precision=HIGHEST)
    return turned * (2.0 / heights).reshape(-1, 1, 1, 1)


def line_slope_width(values, widths, derivative):
    node_count = derivative.shape[0]
    shaped = values.reshape(values.shape[:-2] + (widths.shape[0], node_count, values.shape[-1]))
    turned = jnp.einsum("km,...cmz->...ckz", derivative, shaped, precision=HIGHEST)
    return (turned * (2.0 / widths)[:, None, None]).reshape(values.shape)


def line_slope_span(values, span_slope):
    return jnp.einsum("zw,...w->...z", span_slope, values, precision=HIGHEST)


def line_gradients(values, widths, heights, derivative, span_slope):
    return (
        line_slope_width(values, widths, derivative),
        slope_height(values, heights, derivative),
        line_slope_span(values, span_slope),
    )


def advect(line_values, slopes, base_now, base_slopes):
    pieces = []
    for component in range(3):
        summed = (
            base_now[0] * slopes[0][component]
            + base_now[1] * slopes[1][component]
            + base_now[2] * slopes[2][component]
        )
        summed = summed - (
            line_values[0] * base_slopes[component][0]
            + line_values[1] * base_slopes[component][1]
            + line_values[2] * base_slopes[component][2]
        )
        pieces.append(summed)
    return jnp.stack(pieces)


def assemble_rows(joined, node_count):
    first_row = joined[..., :, 0, :, :]
    last_row = joined[..., :, node_count - 1, :, :]
    shared = last_row[..., :-1, :, :] + first_row[..., 1:, :, :]
    new_first = jnp.concatenate([first_row[..., :1, :, :], shared], axis=-3)
    new_last = jnp.concatenate([shared, last_row[..., -1:, :, :]], axis=-3)
    return jnp.concatenate(
        [
            new_first[..., :, None, :, :],
            joined[..., :, 1 : node_count - 1, :, :],
            new_last[..., :, None, :, :],
        ],
        axis=-3,
    )


def edge_assemble(values, is_first, is_last, node_count):
    extended = padded(values, (("elem", 4),), 1)
    following = extended[..., 2:]
    preceding = extended[..., :-2]
    joined = values + jnp.where(is_last, following, 0.0) + jnp.where(is_first, preceding, 0.0)
    return assemble_rows(joined, node_count)


def inner_product(left, right, weight):
    return jnp.sum(left * right * weight, axis=(-4, -3, -1), keepdims=True)


def paired_products(residual, image_vec, weight):
    return lax.psum(
        (inner_product(residual, residual, weight), inner_product(residual, image_vec, weight)),
        "elem",
    )


def local_general(adjoint_velocity, base_flow, column_widths, row_heights, base_phase):
    node_count = adjoint_velocity.shape[2]
    row_count = adjoint_velocity.shape[1]
    columns_here = column_widths.shape[0]
    part_nodes = columns_here * node_count
    planes_local = adjoint_velocity.shape[3] // part_nodes
    adjoint_local = adjoint_velocity.reshape(3, row_count, node_count, planes_local, part_nodes)
    plane_parts = lax.axis_size("four")
    plane_total = planes_local * plane_parts
    columns_line = columns_here // plane_parts
    line_nodes = columns_line * node_count
    base_local = base_flow.reshape(3, row_count, node_count, line_nodes, plane_total)
    basis_rows, wavenumbers, span_slope = fourier_table(plane_total)
    derivative, weights = gll_tables(node_count)
    wave_local = lax.dynamic_slice_in_dim(
        wavenumbers, lax.axis_index("four") * planes_local, planes_local
    )
    line_widths = lax.dynamic_slice_in_dim(
        column_widths, lax.axis_index("four") * columns_line, columns_line
    )
    node_widths = jnp.repeat(column_widths, node_count)
    node_weights = jnp.tile(weights, columns_here)
    eye_cols = jnp.eye(columns_here, dtype=jnp.float32)
    block_turn = jnp.kron(eye_cols, derivative.T)
    block_back = jnp.kron(eye_cols, derivative)
    base_now = jnp.roll(base_local.astype(jnp.float32), base_phase[0], axis=4)
    base_slopes = line_gradients(base_now, line_widths, row_heights, derivative, span_slope)
    sending = jnp.transpose(adjoint_local, (0, 1, 2, 4, 3))
    arrived = lax.all_to_all(sending, "four", split_axis=3, concat_axis=4, tiled=True)
    line_values = jnp.einsum("jz,...xj->...xz", basis_rows, arrived, precision=HIGHEST)
    slopes = line_gradients(line_values, line_widths, row_heights, derivative, span_slope)
    advection = advect(line_values, slopes, base_now, base_slopes)
    advection_hat = jnp.einsum("jz,...xz->...xj", basis_rows, advection, precision=HIGHEST)
    returned = lax.all_to_all(advection_hat, "four", split_axis=4, concat_axis=3, tiled=True)
    returned = jnp.transpose(returned, (0, 1, 2, 4, 3))
    node_x = jnp.arange(part_nodes, dtype=jnp.int32)
    place_x = node_x % node_count
    is_first = place_x == 0
    is_last = place_x == node_count - 1
    height_b = row_heights.reshape(-1, 1, 1, 1)
    weight_y = weights.reshape(-1, 1, 1)
    source = SIGMA * adjoint_local + returned / NU
    local_side = node_widths * height_b * 0.25 * weight_y * node_weights * source
    right_side = edge_assemble(local_side, is_first, is_last, node_count)
    column_x = lax.axis_index("elem") * columns_here + node_x // node_count
    last_column = columns_here * lax.axis_size("elem") - 1
    shared_x = is_first & (column_x > 0) | is_last & (column_x < last_column)
    node_y = jnp.arange(row_count * node_count, dtype=jnp.int32)
    place_y = node_y % node_count
    row_y = node_y // node_count
    shared_y = (place_y == 0) & (row_y > 0) | (place_y == node_count - 1) & (row_y < row_count - 1)
    mult_x = 1.0 + shared_x.astype(jnp.float32)
    mult_y = 1.0 + shared_y.astype(jnp.float32)
    weight = (1.0 / (mult_y[:, None] * mult_x[None, :])).reshape(
        row_count, node_count, 1, part_nodes
    )
    wave_b = (wave_local * wave_local).reshape(-1, 1)

    def helmholtz(values):
        along_x = jnp.einsum("...n,nm->...m", values, block_turn, precision=HIGHEST) * node_weights
        back_x = jnp.einsum("...n,nm->...m", along_x, block_back, precision=HIGHEST)
        along_y = (
            jnp.einsum("km,...ympx->...ykpx", derivative, values, precision=HIGHEST) * weight_y
        )
        back_y = jnp.einsum("km,...ykpx->...ympx", derivative, along_y, precision=HIGHEST)
        summed = (
            height_b / node_widths * weight_y * back_x
            + node_widths / height_b * node_weights * back_y
        )
        summed = (
            summed
            + (wave_b + SIGMA) * (node_widths * height_b * 0.25) * weight_y * node_weights * values
        )
        return edge_assemble(summed, is_first, is_last, node_count)

    solution = jnp.zeros_like(right_side)
    residual = right_side
    image_vec = helmholtz(residual)
    norm_now, product = paired_products(residual, image_vec, weight)
    step_size = norm_now / product
    direction = residual
    along = image_vec
    for iteration in range(ITERS):
        solution = solution + step_size * direction
        residual = residual - step_size * along
        if iteration + 1 < ITERS:
            image_vec = helmholtz(residual)
            norm_next, product = paired_products(residual, image_vec, weight)
            growth = norm_next / norm_now
            step_size = norm_next / (product - growth * norm_next / step_size)
            direction = residual + growth * direction
            along = image_vec + growth * along
            norm_now = norm_next
    return solution.reshape(3, row_count, node_count, planes_local * part_nodes)


MESH = pl.DeviceIdType.MESH
NODES = 121
PAD = 122
TILES = 61
LANES = 128


def gll_numbers(node_count):
    degree = node_count - 1
    points = np.cos(np.pi * np.arange(node_count) / degree)
    for newton_step in range(60):
        legendre = legendre_values(points, node_count)
        points = points - (points * legendre[:, degree] - legendre[:, degree - 1]) / (
            node_count * legendre[:, degree]
        )
    legendre = legendre_values(points, node_count)
    weights = (2.0 / (degree * node_count * legendre[:, degree] ** 2))[::-1]
    points = points[::-1]
    end_values = legendre[::-1, degree]
    derivative = np.zeros((node_count, node_count))
    for row_index in range(node_count):
        for column in range(node_count):
            if row_index != column:
                derivative[row_index, column] = end_values[row_index] / (
                    end_values[column] * (points[row_index] - points[column])
                )
    derivative[0, 0] = -degree * node_count / 4.0
    derivative[degree, degree] = degree * node_count / 4.0
    derivative = derivative.astype(np.float32).astype(np.float64)
    weights = weights.astype(np.float32).astype(np.float64)
    return derivative, weights


def span_numbers(plane_count):
    positions = np.arange(plane_count)
    basis_rows = np.zeros((plane_count, plane_count))
    basis_rows[0] = 1.0 / np.sqrt(plane_count)
    basis_rows[1] = np.cos(np.pi * positions) / np.sqrt(plane_count)
    for wave_index in range(1, plane_count // 2):
        basis_rows[2 * wave_index] = np.sqrt(2.0 / plane_count) * np.cos(
            2.0 * np.pi * wave_index * positions / plane_count
        )
        basis_rows[2 * wave_index + 1] = np.sqrt(2.0 / plane_count) * np.sin(
            2.0 * np.pi * wave_index * positions / plane_count
        )
    wave_counts = np.arange(plane_count) // 2
    wave_counts[1] = plane_count // 2
    wave_counts[0] = 0
    wavenumbers = 2.0 * np.pi * wave_counts / (plane_count / 64.0)
    rotate = np.zeros((plane_count, plane_count))
    for wave_index in range(1, plane_count // 2):
        rotate[2 * wave_index, 2 * wave_index + 1] = wavenumbers[2 * wave_index]
        rotate[2 * wave_index + 1, 2 * wave_index] = -wavenumbers[2 * wave_index]
    return basis_rows, basis_rows.T @ rotate @ basis_rows


def two_parts(table):
    table = table.astype(np.float32)
    high = table.astype(jnp.bfloat16)
    low = (table - high.astype(np.float32)).astype(jnp.bfloat16)
    return high, low


def split_values(values):
    high = values.astype(jnp.bfloat16)
    low = (values - high.astype(jnp.float32)).astype(jnp.bfloat16)
    return high, low


def three_parts(values):
    high = values.astype(jnp.bfloat16)
    rest = values - high.astype(jnp.float32)
    middle = rest.astype(jnp.bfloat16)
    return high, middle, (rest - middle.astype(jnp.float32)).astype(jnp.bfloat16)


def dot(left, right):
    return jnp.dot(left, right, preferred_element_type=jnp.float32)


def dot_three(values, high, low):
    vh, vl = split_values(values)
    return dot(vh, high) + (dot(vl, high) + dot(vh, low))


def times(matrix, values, sign):
    n = len(values)
    half = n // 2
    even = [values[m] + values[n - 1 - m] for m in range(half)]
    odd = [values[m] - values[n - 1 - m] for m in range(half)]
    out = [None] * n
    for k in range(half + 1):
        s = None
        d = None
        for m in range(half):
            ce = 0.5 * (matrix[k, m] + matrix[k, n - 1 - m])
            co = 0.5 * (matrix[k, m] - matrix[k, n - 1 - m])
            if not (k == half and sign < 0):
                term = float(ce) * even[m]
                s = term if s is None else s + term
            if not (k == half and sign > 0):
                term = float(co) * odd[m]
                d = term if d is None else d + term
        if not (k == half and sign < 0):
            s = s + float(matrix[k, half]) * values[half]
        if k == half:
            out[k] = s if sign > 0 else d
        else:
            out[k] = s + d
            out[n - 1 - k] = s - d if sign > 0 else d - s
    return out


def swap_halves(a, b, low):
    axis = a.ndim - 2
    return (
        jnp.where(low, a, pltpu.roll(b, 4, axis)),
        jnp.where(low, pltpu.roll(a, 4, axis), b),
    )


def chunk_start(step, size, total):
    return jnp.minimum(step * size, total - size)


def section_kernel(
    sizes,
    derivative,
    weights,
    adj_ref,
    flow_ref,
    place_ref,
    wh_ref,
    wl_ref,
    vh_ref,
    vl_ref,
    dh_ref,
    dl_ref,
    widths_ref,
    heights_ref,
    phase_ref,
    wq_ref,
    final_ref,
    coef_ref,
    out_ref,
    base_rows,
    part_a,
    part_b,
    send1,
    recv1,
    send2,
    recv2,
    base_now,
    base_slope,
    lines,
    line_z,
    acc,
    res,
    image,
    direction,
    along,
    edges,
    ghosts,
    sums,
    sums_in,
    send1_sem,
    recv1_sem,
    send2_sem,
    recv2_sem,
    local_sem,
    edge_send_sem,
    edge_recv_sem,
    sum_send_sem,
    sum_recv_sem,
):
    n_four, n_elem = sizes
    q = 11
    elem = lax.axis_index("elem")
    four = lax.axis_index("four")
    stiff = derivative.T @ (weights[:, None] * derivative)

    barrier = pltpu.get_barrier_semaphore()
    for k in range(1, n_four):
        pl.semaphore_signal(
            barrier, inc=1, device_id=(elem, lax.rem(four + k, n_four)), device_id_type=MESH
        )
    for k in range(1, n_elem):
        pl.semaphore_signal(
            barrier, inc=1, device_id=(lax.rem(elem + k, n_elem), four), device_id_type=MESH
        )

    low3 = lax.broadcasted_iota(jnp.int32, (1, 8, LANES), 1) < 4
    low3w = lax.broadcasted_iota(jnp.int32, (1, 8, 256), 1) < 4

    lane16 = lax.broadcasted_iota(jnp.int32, (11, LANES), 1)

    def spread(c):
        for ey in range(2):

            def group(g, carry, ey=ey):
                start = pl.multiple_of(g * 1408, LANES)
                for jl in range(8):
                    w, o = (176 * jl) // LANES, (176 * jl) % LANES
                    tiles = [
                        adj_ref[c, ey, :, pl.ds(start + LANES * min(w + i, 10), LANES)]
                        for i in range(3)
                    ]
                    if o:
                        tiles = [pltpu.roll(x, LANES - o, 1) for x in tiles]
                        keep = lane16 < LANES - o
                        first = jnp.where(keep, tiles[0], tiles[1])
                        second = jnp.where(keep, tiles[1], tiles[2])
                    else:
                        first, second = tiles[0], tiles[1]
                    row = pl.multiple_of((ey * 64 + g * 8 + jl) * 16, 16)
                    part_a[pl.ds(row, 11), :] = first
                    part_b[pl.ds(row, 11), :] = second
                return carry

            lax.fori_loop(0, 8, group, 0)

        def turn(qy, carry):
            rows = pl.ds(qy, 128, stride=16)
            block = jnp.concatenate([part_a[rows, :], part_b[rows, :]], axis=1)
            total = None
            for piece in three_parts(block):
                term = lax.dot_general(
                    place_ref[...],
                    piece,
                    (((1,), (1,)), ((), ())),
                    preferred_element_type=jnp.float32,
                )
                total = term if total is None else total + term
            coef_ref[c, pl.ds(qy * 11, 11)] = total.reshape(11, 16, LANES)
            return carry

        lax.fori_loop(0, 11, turn, 0)
        coef_ref[c, NODES] = jnp.zeros((16, LANES), jnp.float32)

    def gather(c):
        def turn(qy, carry):
            block = out_ref[c, pl.ds(qy * 11, 11)].reshape(176, LANES)
            block = jnp.concatenate([block, jnp.zeros((80, LANES), jnp.float32)], axis=0).T
            total = None
            for piece in three_parts(block):
                term = dot(piece[:, :176], place_ref[...])
                total = term if total is None else total + term
            rows = pl.ds(qy, 128, stride=16)
            part_a[rows, :] = total[:, :LANES]
            part_b[rows, :] = total[:, LANES:]
            return carry

        lax.fori_loop(0, 11, turn, 0)
        for ey in range(2):

            def group(g, carry, ey=ey):
                start = pl.multiple_of(g * 1408, LANES)
                sources = []
                for jl in range(8):
                    row = pl.multiple_of((ey * 64 + g * 8 + jl) * 16, 16)
                    sources.append((part_a[pl.ds(row, 11), :], part_b[pl.ds(row, 11), :]))
                for w in range(11):
                    done = None
                    at = 0
                    while at < LANES:
                        jl, node = divmod(LANES * w + at, 176)
                        side = 0 if node < LANES else 1
                        length = min((LANES if side == 0 else 176) - node, LANES - at)
                        value = sources[jl][side]
                        move = (at - (node - LANES * side)) % LANES
                        if move:
                            value = pltpu.roll(value, move, 1)
                        done = value if done is None else jnp.where(lane16 < at, done, value)
                        at += length
                    final_ref[c, ey, :, pl.ds(start + LANES * w, LANES)] = done
                return carry

            lax.fori_loop(0, 8, group, 0)

    def pack(c):
        def body(step, carry):
            t = chunk_start(step, 8, TILES)
            for tile in range(2):
                a = coef_ref[c, pl.ds(t, 8), pl.ds(8 * tile, 8), :]
                b = coef_ref[c, pl.ds(t + TILES, 8), pl.ds(8 * tile, 8), :]
                first, second = swap_halves(a, b, low3)
                send1[2 * tile, c, pl.ds(t, 8)] = first
                send1[2 * tile + 1, c, pl.ds(t, 8)] = second
            return carry

        lax.fori_loop(0, 8, body, 0)

    def exchange(source, target, send_sem, recv_sem, c):
        return [
            pltpu.make_async_remote_copy(
                src_ref=source.at[lax.rem(four + k, n_four), c],
                dst_ref=target.at[four, c],
                send_sem=send_sem.at[c, k],
                recv_sem=recv_sem.at[c, k],
                device_id=(elem, lax.rem(four + k, n_four)),
                device_id_type=MESH,
            )
            for k in range(1, n_four)
        ]

    def own(source, target, c, which):
        return pltpu.make_async_copy(source.at[four, c], target.at[four, c], local_sem.at[which, c])

    copies1 = [exchange(send1, recv1, send1_sem, recv1_sem, c) for c in range(3)]
    own1 = [own(send1, recv1, c, 0) for c in range(3)]
    copies2 = [exchange(send2, recv2, send2_sem, recv2_sem, c) for c in range(3)]
    own2 = [own(send2, recv2, c, 1) for c in range(3)]

    spread(0)
    pack(0)
    pl.semaphore_wait(barrier, n_four - 1 + n_elem - 1)
    for copy in copies1[0]:
        copy.start()
    own1[0].start()
    for c in (1, 2):
        spread(c)
        pack(c)
        for copy in copies1[c]:
            copy.start()
        own1[c].start()

    row_w = lax.broadcasted_iota(jnp.int32, (8, LANES), 0)
    first_column = four * 4
    hx = jnp.zeros((8, LANES), jnp.float32)
    hy = jnp.zeros((8, LANES), jnp.float32)
    for i in range(8):
        hx = jnp.where(row_w == i, widths_ref[first_column + i % 4], hx)
        hy = jnp.where(row_w == i, heights_ref[i // 4], hy)
    gx = 2.0 / hx
    gy = 2.0 / hy

    phase = phase_ref[0]
    shift_row = lax.broadcasted_iota(jnp.int32, (256, 256), 0)
    shift_col = lax.broadcasted_iota(jnp.int32, (256, 256), 1)
    moved = jnp.where(shift_row + phase >= 256, shift_row + phase - 256, shift_row + phase)
    shift = jnp.where(moved == shift_col, 1.0, 0.0).astype(jnp.bfloat16)

    for c in range(3):

        def place_body(qx, carry, c=c):
            for ex in range(4):
                start = pl.multiple_of((ex * 11 + qx) * 256, 256)
                for ey in range(2):
                    piece = flow_ref[c, ey, :, pl.ds(start, 256)].astype(jnp.float32)
                    row = qx * 8 + ey * 4 + ex
                    base_rows[0, pl.ds(row, 11, stride=88), :] = piece[:, :LANES]
                    base_rows[1, pl.ds(row, 11, stride=88), :] = piece[:, LANES:]
            return carry

        lax.fori_loop(0, 11, place_body, 0)

        def roll_body(step, carry, c=c):
            n = step * 11
            at = pl.ds(pl.multiple_of(n * 8, 8), 88)
            rows = jnp.concatenate([base_rows[0, at, :], base_rows[1, at, :]], axis=1)
            now = dot(rows.astype(jnp.bfloat16), shift)
            base_now[c, pl.ds(n, 11)] = now.reshape(11, 8, 256)
            now_b = now.astype(jnp.bfloat16)
            slope = dot(now_b, dh_ref[...]) + dot(now_b, dl_ref[...])
            base_slope[c, 2, pl.ds(n, 11)] = slope.reshape(11, 8, 256)
            return carry

        lax.fori_loop(0, 11, roll_body, 0)

        def slope_body(step, carry, c=c):
            for h in range(2):
                part = pl.ds(LANES * h, LANES)
                turned = times(
                    derivative, [base_now[c, step * 11 + m, :, part] for m in range(q)], -1
                )
                for k in range(q):
                    base_slope[c, 0, step * 11 + k, :, part] = gx * turned[k]
                turned = times(
                    derivative, [base_now[c, m * 11 + step, :, part] for m in range(q)], -1
                )
                for k in range(q):
                    base_slope[c, 1, k * 11 + step, :, part] = gy * turned[k]
            return carry

        lax.fori_loop(0, 11, slope_body, 0)

    for c in range(3):
        acc[c, NODES] = jnp.zeros((8, 256), jnp.float32)
    edges[...] = jnp.zeros(edges.shape, jnp.float32)
    sums[...] = jnp.zeros(sums.shape, jnp.float32)

    for c in range(3):
        for copy in copies1[c]:
            copy.wait_recv()
        own1[c].wait()

        def line_body(step, carry, c=c):
            t = chunk_start(step, 8, TILES)
            out = None
            for s in range(n_four):
                rows = recv1[s, c, pl.ds(t, 8)].reshape(64, LANES)
                part = dot_three(
                    rows, wh_ref[pl.ds(s * LANES, LANES), :], wl_ref[pl.ds(s * LANES, LANES), :]
                )
                out = part if out is None else out + part
            e0 = out[:, :256].reshape(8, 8, 256)
            e1 = out[:, 256:].reshape(8, 8, 256)
            a, b = swap_halves(e0, e1, low3w)
            lines[pl.ds(t, 8)] = a
            lines[pl.ds(t + TILES, 8)] = b
            return carry

        lax.fori_loop(0, 8, line_body, 0)

        def span_body(step, carry):
            n = step * 11
            rows = lines[pl.ds(n, 11)].reshape(88, 256)
            line_z[pl.ds(n, 11)] = dot_three(rows, dh_ref[...], dl_ref[...]).reshape(11, 8, 256)
            return carry

        lax.fori_loop(0, 11, span_body, 0)

        def add_x(step, carry, c=c):
            for h in range(2):
                part = pl.ds(LANES * h, LANES)
                values = [lines[step * 11 + m, :, part] for m in range(q)]
                turned = times(derivative, values, -1)
                for k in range(q):
                    n = step * 11 + k
                    gain = base_now[0, n, :, part] * (gx * turned[k])
                    gain = gain + base_now[2, n, :, part] * line_z[n, :, part]
                    for e in range(3):
                        change = -values[k] * base_slope[c, e, n, :, part]
                        if e == c:
                            change = change + gain
                        if c > 0:
                            change = change + acc[e, n, :, part]
                        acc[e, n, :, part] = change
            return carry

        lax.fori_loop(0, 11, add_x, 0)

        def add_y(step, carry, c=c):
            for h in range(2):
                part = pl.ds(LANES * h, LANES)
                values = [lines[m * 11 + step, :, part] for m in range(q)]
                turned = times(derivative, values, -1)
                for k in range(q):
                    n = k * 11 + step
                    acc[c, n, :, part] += base_now[1, n, :, part] * (gy * turned[k])
            return carry

        lax.fori_loop(0, 11, add_y, 0)

    for c in range(3):

        def back_body(step, carry, c=c):
            t = chunk_start(step, 8, TILES)
            a = acc[c, pl.ds(t, 8)]
            b = acc[c, pl.ds(t + TILES, 8)]
            e0, e1 = swap_halves(a, b, low3w)
            e0 = e0.reshape(64, 256)
            e1 = e1.reshape(64, 256)
            out = dot_three(e0, vh_ref[pl.ds(0, 256), :], vl_ref[pl.ds(0, 256), :])
            out = out + dot_three(e1, vh_ref[pl.ds(256, 256), :], vl_ref[pl.ds(256, 256), :])
            for s in range(n_four):
                send2[s, c, pl.ds(t, 8)] = out[:, LANES * s : LANES * (s + 1)].reshape(8, 8, LANES)
            return carry

        lax.fori_loop(0, 8, back_body, 0)
        for copy in copies2[c]:
            copy.start()
        own2[c].start()

    lane = lax.broadcasted_iota(jnp.int32, (8, LANES), 1)
    row = lax.broadcasted_iota(jnp.int32, (8, LANES), 0)
    lower = lane < 64
    lane_plane = jnp.where(lower, lane, lane - 64) + four * 64
    kappa = lane_plane // 2
    kappa = jnp.where(lane_plane == 1, 32 * n_four, kappa)
    kappa = jnp.where(lane_plane == 0, 0, kappa)
    beta = kappa.astype(jnp.float32) * np.float32(2.0 * np.pi / n_four)
    wave = beta * beta + SIGMA
    hyl = jnp.where(lower, heights_ref[0], heights_ref[1])
    hxl = []
    for tile in range(2):
        h = jnp.zeros((8, LANES), jnp.float32)
        for i in range(8):
            h = jnp.where(row == i, widths_ref[8 * tile + i], h)
        hxl.append(h)
    quarter = [0.25 * h * hyl for h in hxl]
    scale_x = [hyl / h for h in hxl]
    scale_y = [h / hyl for h in hxl]
    one = jnp.ones((8, LANES), jnp.float32)
    half = 0.5 * one
    left_inner = elem > 0
    right_inner = elem < n_elem - 1
    share_first = [jnp.where(jnp.logical_and(row == 0, jnp.logical_not(left_inner)), one, half), half]
    share_last = [half, jnp.where(jnp.logical_and(row == 7, jnp.logical_not(right_inner)), one, half)]
    share_top = jnp.where(lower, one, half)
    share_bottom = jnp.where(lower, half, one)
    right = lax.rem(elem + 1, n_elem)
    left = lax.rem(elem + n_elem - 1, n_elem)

    def edge_copies(c, level):
        return [
            pltpu.make_async_remote_copy(
                src_ref=edges.at[c, level, 0],
                dst_ref=ghosts.at[c, level, 1],
                send_sem=edge_send_sem.at[c, level, 0],
                recv_sem=edge_recv_sem.at[c, level, 1],
                device_id=(left, four),
                device_id_type=MESH,
            ),
            pltpu.make_async_remote_copy(
                src_ref=edges.at[c, level, 1],
                dst_ref=ghosts.at[c, level, 0],
                send_sem=edge_send_sem.at[c, level, 1],
                recv_sem=edge_recv_sem.at[c, level, 0],
                device_id=(right, four),
                device_id_type=MESH,
            ),
        ]

    def edge_start(values, c, level):
        for qy in range(q):
            edges[c, level, 0, pl.ds(qy, 1), :] = values[qy * 11, pl.ds(0, 1), :]
            edges[c, level, 1, pl.ds(qy, 1), :] = values[qy * 11 + 10, pl.ds(15, 1), :]
        copies = edge_copies(c, level)
        for copy in copies:
            copy.start()
        return copies

    left_keep = jnp.where(left_inner, 1.0, 0.0)
    right_keep = jnp.where(right_inner, 1.0, 0.0)

    def assemble_here(values, c, level, copies):
        for copy in copies:
            copy.wait_recv()

        def body(qy, carry):
            n0 = qy * 11
            a0 = values[n0, pl.ds(0, 8), :]
            a1 = values[n0, pl.ds(8, 8), :]
            b0 = values[n0 + 10, pl.ds(0, 8), :]
            b1 = values[n0 + 10, pl.ds(8, 8), :]
            from_left = ghosts[c, level, 0, pl.ds(qy, 1), :] * left_keep
            from_right = ghosts[c, level, 1, pl.ds(qy, 1), :] * right_keep
            rb0 = pltpu.roll(b0, 1, 0)
            rb1 = pltpu.roll(b1, 1, 0)
            ra0 = pltpu.roll(a0, 7, 0)
            ra1 = pltpu.roll(a1, 7, 0)
            values[n0, pl.ds(0, 8), :] = a0 + jnp.where(row == 0, from_left, rb0)
            values[n0, pl.ds(8, 8), :] = a1 + jnp.where(row == 0, rb0, rb1)
            values[n0 + 10, pl.ds(0, 8), :] = b0 + jnp.where(row == 7, ra1, ra0)
            values[n0 + 10, pl.ds(8, 8), :] = b1 + jnp.where(row == 7, from_right, ra1)
            return carry

        lax.fori_loop(0, q, body, 0)
        for qx in range(q):
            for tile in range(2):
                rows = pl.ds(8 * tile, 8)
                top = values[qx, rows, :]
                bottom = values[110 + qx, rows, :]
                values[qx, rows, :] = top + jnp.where(lower, 0.0, pltpu.roll(bottom, 64, 1))
                values[110 + qx, rows, :] = bottom + jnp.where(lower, pltpu.roll(top, 64, 1), 0.0)

    def sum_copies(c, level):
        return [
            pltpu.make_async_remote_copy(
                src_ref=sums.at[c, level],
                dst_ref=sums_in.at[c, level, k],
                send_sem=sum_send_sem.at[c, level, k],
                recv_sem=sum_recv_sem.at[c, level, k],
                device_id=(lax.rem(elem + k, n_elem), four),
                device_id_type=MESH,
            )
            for k in range(1, n_elem)
        ]

    zero = jnp.zeros((8, LANES), jnp.float32)

    def apply(values, target):
        def body_x(qy, carry):
            rr, wy = carry[0], wq_ref[qy]
            share = jnp.where(qy == 0, share_top, jnp.where(qy == q - 1, share_bottom, one))
            for tile in range(2):
                rows = pl.ds(8 * tile, 8)
                v = [values[qy * 11 + m, rows, :] for m in range(q)]
                turned = times(stiff, v, 1)
                ax = scale_x[tile] * wy
                mass = (wave * quarter[tile]) * wy
                inner = None
                for k in range(q):
                    target[qy * 11 + k, rows, :] = ax * turned[k] + (mass * float(weights[k])) * v[k]
                    square = v[k] * v[k]
                    if k == 0:
                        square = square * share_first[tile]
                    if k == q - 1:
                        square = square * share_last[tile]
                    inner = square if inner is None else inner + square
                rr = rr + share * inner
            return (rr,)

        (rr,) = lax.fori_loop(0, q, body_x, (zero,))

        def body_y(qx, carry):
            product, wx = carry[0], wq_ref[qx]
            for tile in range(2):
                rows = pl.ds(8 * tile, 8)
                v = [values[m * 11 + qx, rows, :] for m in range(q)]
                turned = times(stiff, v, 1)
                ay = scale_y[tile] * wx
                for k in range(q):
                    total = target[k * 11 + qx, rows, :] + ay * turned[k]
                    target[k * 11 + qx, rows, :] = total
                    product = product + v[k] * total
            return (product,)

        (product,) = lax.fori_loop(0, q, body_y, (zero,))
        return rr, product

    def fold(values):
        total = jnp.sum(values, axis=0, keepdims=True)
        return total + pltpu.roll(total, 64, 1)

    waiting = []
    for c in range(3):
        for copy in copies2[c]:
            copy.wait_recv()
        own2[c].wait()

        def unpack_body(step, carry, c=c):
            t = chunk_start(step, 8, TILES)
            for tile in range(2):
                rows = pl.ds(8 * tile, 8)
                a, b = swap_halves(
                    recv2[2 * tile, c, pl.ds(t, 8)], recv2[2 * tile + 1, c, pl.ds(t, 8)], low3
                )
                res[pl.ds(t, 8), rows, :] = SIGMA * coef_ref[c, pl.ds(t, 8), rows, :] + a / NU
                res[pl.ds(t + TILES, 8), rows, :] = (
                    SIGMA * coef_ref[c, pl.ds(t + TILES, 8), rows, :] + b / NU
                )
            return carry

        lax.fori_loop(0, 8, unpack_body, 0)

        def mass_body(qy, carry):
            wy = wq_ref[qy]
            for tile in range(2):
                rows = pl.ds(8 * tile, 8)
                area = quarter[tile] * wy
                for k in range(q):
                    res[qy * 11 + k, rows, :] = res[qy * 11 + k, rows, :] * (area * float(weights[k]))
            return carry

        lax.fori_loop(0, q, mass_body, 0)
        copies = edge_start(res, c, 0)
        waiting += copies
        assemble_here(res, c, 0, copies)

        norm_now = None
        step_size = None
        for it in range(ITERS):
            rr, product = apply(res, image)
            sums[c, it, pl.ds(0, 1), :] = fold(rr)
            sums[c, it, pl.ds(1, 1), :] = fold(product)
            sum_list = sum_copies(c, it)
            for copy in sum_list:
                copy.start()
            waiting += sum_list
            if it + 1 < ITERS:
                copies = edge_start(image, c, it + 1)
                waiting += copies
                assemble_here(image, c, it + 1, copies)
            for copy in sum_list:
                copy.wait_recv()
            total = sums[c, it]
            for k in range(1, n_elem):
                total = total + sums_in[c, it, k]
            norm_next = total[0:1, :]
            product = total[1:2, :]
            if it == 0:
                growth = jnp.zeros_like(norm_next)
                step_size = norm_next / product
            else:
                growth = norm_next / norm_now
                step_size = norm_next / (product - growth * norm_next / step_size)
            norm_now = norm_next

            def update(n, carry, it=it, c=c, growth=growth, step_size=step_size):
                for j in range(11):
                    m = n * 11 + j
                    r = res[m]
                    if it == 0:
                        d = r
                        out_ref[c, m] = step_size * d
                    else:
                        d = r + growth * direction[m]
                        out_ref[c, m] = out_ref[c, m] + step_size * d
                    if it + 1 < ITERS:
                        direction[m] = d
                        a = image[m]
                        if it > 0:
                            a = a + growth * along[m]
                        if it + 2 < ITERS:
                            along[m] = a
                        res[m] = r - step_size * a
                return carry

            lax.fori_loop(0, 11, update, 0)
        gather(c)

    for group in copies1 + copies2 + [waiting]:
        for copy in group:
            copy.wait_send()


def local_blocks(adjoint_velocity, base_flow, column_widths, row_heights, base_phase):
    n_four, n_elem = lax.axis_size("four"), lax.axis_size("elem")
    derivative, weights = gll_numbers(11)
    basis_rows, span_slope = span_numbers(256)
    forward = np.zeros((n_four, 2, 64, 2, 256))
    for ey in range(2):
        forward[:, ey, :, ey, :] = basis_rows.reshape(n_four, 64, 256)
    forward = forward.reshape(512, 512)
    tables = two_parts(forward) + two_parts(forward.T) + two_parts(span_slope.T)
    place = np.zeros((11, 16, 256), np.float32)
    for column in range(16):
        for qx in range(11):
            place[qx, column, column * 11 + qx] = 1.0
    place = place.reshape(176, 256).astype(jnp.bfloat16)
    vmem = pl.BlockSpec(memory_space=pltpu.VMEM)
    smem = pl.BlockSpec(memory_space=pltpu.SMEM)
    f32 = jnp.float32
    blocks = (n_four, 3, TILES, 8, LANES)
    field = (PAD, 16, LANES)
    dma = pltpu.SemaphoreType.DMA
    out = pl.pallas_call(
        lambda *refs: section_kernel((n_four, n_elem), derivative, weights, *refs),
        out_shape=jax.ShapeDtypeStruct(adjoint_velocity.shape, f32),
        in_specs=[vmem] * 9 + [smem] * 4,
        out_specs=vmem,
        scratch_shapes=[
            pltpu.VMEM((3, PAD, 16, LANES), f32),
            pltpu.VMEM((3, NODES, 16, LANES), f32),
            pltpu.VMEM((2, NODES * 8, LANES), f32),
            pltpu.VMEM((2048, LANES), f32),
            pltpu.VMEM((2048, LANES), f32),
            pltpu.VMEM(blocks, f32),
            pltpu.VMEM(blocks, f32),
            pltpu.VMEM(blocks, f32),
            pltpu.VMEM(blocks, f32),
            pltpu.VMEM((3, NODES, 8, 256), f32),
            pltpu.VMEM((3, 3, NODES, 8, 256), f32),
            pltpu.VMEM((PAD, 8, 256), f32),
            pltpu.VMEM((PAD, 8, 256), f32),
            pltpu.VMEM((3, PAD, 8, 256), f32),
            pltpu.VMEM(field, f32),
            pltpu.VMEM(field, f32),
            pltpu.VMEM(field, f32),
            pltpu.VMEM(field, f32),
            pltpu.VMEM((3, ITERS, 2, 16, LANES), f32),
            pltpu.VMEM((3, ITERS, 2, 16, LANES), f32),
            pltpu.VMEM((3, ITERS, 8, LANES), f32),
            pltpu.VMEM((3, ITERS, n_elem, 8, LANES), f32),
            dma((3, n_four)),
            dma((3, n_four)),
            dma((3, n_four)),
            dma((3, n_four)),
            dma((2, 3)),
            dma((3, ITERS, 2)),
            dma((3, ITERS, 2)),
            dma((3, ITERS, n_elem)),
            dma((3, ITERS, n_elem)),
        ],
        compiler_params=pltpu.CompilerParams(
            collective_id=0, has_side_effects=True, vmem_limit_bytes=60 * 1024 * 1024
        ),
    )(adjoint_velocity, base_flow, place, *tables, column_widths, row_heights, base_phase, weights.astype(np.float32))
    return out


def local(adjoint_velocity, base_flow, column_widths, row_heights, base_phase):
    four, elem = lax.axis_size("four"), lax.axis_size("elem")
    known = (
        adjoint_velocity.shape == (3, 2, 11, 64 * 16 * 11)
        and column_widths.shape == (16,)
        and four == 4
        and elem > 2
    )
    chosen = local_blocks if known else local_general
    return chosen(adjoint_velocity, base_flow, column_widths, row_heights, base_phase)


def solution(mesh):
    return jax.shard_map(
        local,
        mesh=mesh,
        in_specs=(
            P(None, None, None, ("elem", "four")),
            P(None, None, None, ("elem", "four")),
            P("elem"),
            P(),
            P(),
        ),
        out_specs=P(None, None, None, ("elem", "four")),
        check_vma=False,
    )
```

```python
import functools
import jax
import jax.numpy as jnp
import numpy as np
from jax import lax
from jax.experimental import pallas as pl
from jax.experimental.pallas import tpu as pltpu
from jax.sharding import PartitionSpec as P

ITERS = 3


NU = 0.005
DT = 0.01
SIGMA = 1.0 / (NU * DT)
HIGHEST = lax.Precision.HIGHEST


def padded(x, sides, width):
    for axis, dim in sides:
        count, length = (lax.axis_size(axis), x.shape[dim])
        up = [(i, (i + 1) % count) for i in range(count - 1)]
        down = [(j, i) for i, j in up]
        last = lax.slice_in_dim(x, length - width, length, axis=dim)
        first = lax.slice_in_dim(x, 0, width, axis=dim)
        before = lax.ppermute(last, axis, up)
        after = lax.ppermute(first, axis, down)
        x = jnp.concatenate([before, x, after], axis=dim)
    return x


def legendre_values(points, node_count):
    table_rows = np.zeros((points.shape[0], node_count))
    table_rows[:, 0] = 1.0
    table_rows[:, 1] = points
    for degree_now in range(2, node_count):
        table_rows[:, degree_now] = (
            (2 * degree_now - 1) * points * table_rows[:, degree_now - 1]
            - (degree_now - 1) * table_rows[:, degree_now - 2]
        ) / degree_now
    return table_rows


def gll_tables(node_count):
    degree = node_count - 1
    points = np.cos(np.pi * np.arange(node_count) / degree)
    for newton_step in range(60):
        legendre = legendre_values(points, node_count)
        points = points - (points * legendre[:, degree] - legendre[:, degree - 1]) / (
            node_count * legendre[:, degree]
        )
    legendre = legendre_values(points, node_count)
    weights = 2.0 / (degree * node_count * legendre[:, degree] ** 2)
    points = points[::-1]
    weights = weights[::-1]
    end_values = legendre[::-1, degree]
    derivative = np.zeros((node_count, node_count))
    for row_index in range(node_count):
        for column in range(node_count):
            if row_index != column:
                derivative[row_index, column] = end_values[row_index] / (
                    end_values[column] * (points[row_index] - points[column])
                )
    derivative[0, 0] = -degree * node_count / 4.0
    derivative[degree, degree] = degree * node_count / 4.0
    return (jnp.asarray(derivative.astype(np.float32)), jnp.asarray(weights.astype(np.float32)))


def fourier_table(plane_count):
    positions = np.arange(plane_count)
    basis_rows = np.zeros((plane_count, plane_count))
    basis_rows[0] = 1.0 / np.sqrt(plane_count)
    basis_rows[1] = np.cos(np.pi * positions) / np.sqrt(plane_count)
    for wave_index in range(1, plane_count // 2):
        basis_rows[2 * wave_index] = np.sqrt(2.0 / plane_count) * np.cos(
            2.0 * np.pi * wave_index * positions / plane_count
        )
        basis_rows[2 * wave_index + 1] = np.sqrt(2.0 / plane_count) * np.sin(
            2.0 * np.pi * wave_index * positions / plane_count
        )
    wave_counts = np.arange(plane_count) // 2
    wave_counts[1] = plane_count // 2
    wave_counts[0] = 0
    wavenumbers = 2.0 * np.pi * wave_counts / (plane_count / 64.0)
    rotate = np.zeros((plane_count, plane_count))
    for wave_index in range(1, plane_count // 2):
        rotate[2 * wave_index, 2 * wave_index + 1] = wavenumbers[2 * wave_index]
        rotate[2 * wave_index + 1, 2 * wave_index] = -wavenumbers[2 * wave_index]
    span_slope = basis_rows.T @ rotate @ basis_rows
    return (
        jnp.asarray(basis_rows.astype(np.float32)),
        jnp.asarray(wavenumbers.astype(np.float32)),
        jnp.asarray(span_slope.astype(np.float32)),
    )


def slope_height(values, heights, derivative):
    turned = jnp.einsum("km,...ympx->...ykpx", derivative, values, precision=HIGHEST)
    return turned * (2.0 / heights).reshape(-1, 1, 1, 1)


def line_slope_width(values, widths, derivative):
    node_count = derivative.shape[0]
    shaped = values.reshape(values.shape[:-2] + (widths.shape[0], node_count, values.shape[-1]))
    turned = jnp.einsum("km,...cmz->...ckz", derivative, shaped, precision=HIGHEST)
    return (turned * (2.0 / widths)[:, None, None]).reshape(values.shape)


def line_slope_span(values, span_slope):
    return jnp.einsum("zw,...w->...z", span_slope, values, precision=HIGHEST)


def line_gradients(values, widths, heights, derivative, span_slope):
    return (
        line_slope_width(values, widths, derivative),
        slope_height(values, heights, derivative),
        line_slope_span(values, span_slope),
    )


def advect(line_values, slopes, base_now, base_slopes):
    pieces = []
    for component in range(3):
        summed = (
            base_now[0] * slopes[0][component]
            + base_now[1] * slopes[1][component]
            + base_now[2] * slopes[2][component]
        )
        summed = summed - (
            line_values[0] * base_slopes[component][0]
            + line_values[1] * base_slopes[component][1]
            + line_values[2] * base_slopes[component][2]
        )
        pieces.append(summed)
    return jnp.stack(pieces)


def assemble_rows(joined, node_count):
    first_row = joined[..., :, 0, :, :]
    last_row = joined[..., :, node_count - 1, :, :]
    shared = last_row[..., :-1, :, :] + first_row[..., 1:, :, :]
    new_first = jnp.concatenate([first_row[..., :1, :, :], shared], axis=-3)
    new_last = jnp.concatenate([shared, last_row[..., -1:, :, :]], axis=-3)
    return jnp.concatenate(
        [
            new_first[..., :, None, :, :],
            joined[..., :, 1 : node_count - 1, :, :],
            new_last[..., :, None, :, :],
        ],
        axis=-3,
    )


def edge_assemble(values, is_first, is_last, node_count):
    extended = padded(values, (("elem", 4),), 1)
    following = extended[..., 2:]
    preceding = extended[..., :-2]
    joined = values + jnp.where(is_last, following, 0.0) + jnp.where(is_first, preceding, 0.0)
    return assemble_rows(joined, node_count)


def inner_product(left, right, weight):
    return jnp.sum(left * right * weight, axis=(-4, -3, -1), keepdims=True)


def paired_products(residual, image_vec, weight):
    return lax.psum(
        (inner_product(residual, residual, weight), inner_product(residual, image_vec, weight)),
        "elem",
    )


def local_general(adjoint_velocity, base_flow, column_widths, row_heights, base_phase):
    node_count = adjoint_velocity.shape[2]
    row_count = adjoint_velocity.shape[1]
    columns_here = column_widths.shape[0]
    part_nodes = columns_here * node_count
    planes_local = adjoint_velocity.shape[3] // part_nodes
    adjoint_local = adjoint_velocity.reshape(3, row_count, node_count, planes_local, part_nodes)
    plane_parts = lax.axis_size("four")
    plane_total = planes_local * plane_parts
    columns_line = columns_here // plane_parts
    line_nodes = columns_line * node_count
    base_local = base_flow.reshape(3, row_count, node_count, line_nodes, plane_total)
    basis_rows, wavenumbers, span_slope = fourier_table(plane_total)
    derivative, weights = gll_tables(node_count)
    wave_local = lax.dynamic_slice_in_dim(
        wavenumbers, lax.axis_index("four") * planes_local, planes_local
    )
    line_widths = lax.dynamic_slice_in_dim(
        column_widths, lax.axis_index("four") * columns_line, columns_line
    )
    node_widths = jnp.repeat(column_widths, node_count)
    node_weights = jnp.tile(weights, columns_here)
    eye_cols = jnp.eye(columns_here, dtype=jnp.float32)
    block_turn = jnp.kron(eye_cols, derivative.T)
    block_back = jnp.kron(eye_cols, derivative)
    base_now = jnp.roll(base_local.astype(jnp.float32), base_phase[0], axis=4)
    base_slopes = line_gradients(base_now, line_widths, row_heights, derivative, span_slope)
    sending = jnp.transpose(adjoint_local, (0, 1, 2, 4, 3))
    arrived = lax.all_to_all(sending, "four", split_axis=3, concat_axis=4, tiled=True)
    line_values = jnp.einsum("jz,...xj->...xz", basis_rows, arrived, precision=HIGHEST)
    slopes = line_gradients(line_values, line_widths, row_heights, derivative, span_slope)
    advection = advect(line_values, slopes, base_now, base_slopes)
    advection_hat = jnp.einsum("jz,...xz->...xj", basis_rows, advection, precision=HIGHEST)
    returned = lax.all_to_all(advection_hat, "four", split_axis=4, concat_axis=3, tiled=True)
    returned = jnp.transpose(returned, (0, 1, 2, 4, 3))
    node_x = jnp.arange(part_nodes, dtype=jnp.int32)
    place_x = node_x % node_count
    is_first = place_x == 0
    is_last = place_x == node_count - 1
    height_b = row_heights.reshape(-1, 1, 1, 1)
    weight_y = weights.reshape(-1, 1, 1)
    source = SIGMA * adjoint_local + returned / NU
    local_side = node_widths * height_b * 0.25 * weight_y * node_weights * source
    right_side = edge_assemble(local_side, is_first, is_last, node_count)
    column_x = lax.axis_index("elem") * columns_here + node_x // node_count
    last_column = columns_here * lax.axis_size("elem") - 1
    shared_x = is_first & (column_x > 0) | is_last & (column_x < last_column)
    node_y = jnp.arange(row_count * node_count, dtype=jnp.int32)
    place_y = node_y % node_count
    row_y = node_y // node_count
    shared_y = (place_y == 0) & (row_y > 0) | (place_y == node_count - 1) & (row_y < row_count - 1)
    mult_x = 1.0 + shared_x.astype(jnp.float32)
    mult_y = 1.0 + shared_y.astype(jnp.float32)
    weight = (1.0 / (mult_y[:, None] * mult_x[None, :])).reshape(
        row_count, node_count, 1, part_nodes
    )
    wave_b = (wave_local * wave_local).reshape(-1, 1)

    def helmholtz(values):
        along_x = jnp.einsum("...n,nm->...m", values, block_turn, precision=HIGHEST) * node_weights
        back_x = jnp.einsum("...n,nm->...m", along_x, block_back, precision=HIGHEST)
        along_y = (
            jnp.einsum("km,...ympx->...ykpx", derivative, values, precision=HIGHEST) * weight_y
        )
        back_y = jnp.einsum("km,...ykpx->...ympx", derivative, along_y, precision=HIGHEST)
        summed = (
            height_b / node_widths * weight_y * back_x
            + node_widths / height_b * node_weights * back_y
        )
        summed = (
            summed
            + (wave_b + SIGMA) * (node_widths * height_b * 0.25) * weight_y * node_weights * values
        )
        return edge_assemble(summed, is_first, is_last, node_count)

    solution = jnp.zeros_like(right_side)
    residual = right_side
    image_vec = helmholtz(residual)
    norm_now, product = paired_products(residual, image_vec, weight)
    step_size = norm_now / product
    direction = residual
    along = image_vec
    for iteration in range(ITERS):
        solution = solution + step_size * direction
        residual = residual - step_size * along
        if iteration + 1 < ITERS:
            image_vec = helmholtz(residual)
            norm_next, product = paired_products(residual, image_vec, weight)
            growth = norm_next / norm_now
            step_size = norm_next / (product - growth * norm_next / step_size)
            direction = residual + growth * direction
            along = image_vec + growth * along
            norm_now = norm_next
    return solution.reshape(3, row_count, node_count, planes_local * part_nodes)


MESH = pl.DeviceIdType.MESH
NODES = 121
PAD = 122
TILES = 61
LANES = 128


def gll_numbers(node_count):
    degree = node_count - 1
    points = np.cos(np.pi * np.arange(node_count) / degree)
    for newton_step in range(60):
        legendre = legendre_values(points, node_count)
        points = points - (points * legendre[:, degree] - legendre[:, degree - 1]) / (
            node_count * legendre[:, degree]
        )
    legendre = legendre_values(points, node_count)
    weights = (2.0 / (degree * node_count * legendre[:, degree] ** 2))[::-1]
    points = points[::-1]
    end_values = legendre[::-1, degree]
    derivative = np.zeros((node_count, node_count))
    for row_index in range(node_count):
        for column in range(node_count):
            if row_index != column:
                derivative[row_index, column] = end_values[row_index] / (
                    end_values[column] * (points[row_index] - points[column])
                )
    derivative[0, 0] = -degree * node_count / 4.0
    derivative[degree, degree] = degree * node_count / 4.0
    derivative = derivative.astype(np.float32).astype(np.float64)
    weights = weights.astype(np.float32).astype(np.float64)
    return derivative, weights


def span_numbers(plane_count):
    positions = np.arange(plane_count)
    basis_rows = np.zeros((plane_count, plane_count))
    basis_rows[0] = 1.0 / np.sqrt(plane_count)
    basis_rows[1] = np.cos(np.pi * positions) / np.sqrt(plane_count)
    for wave_index in range(1, plane_count // 2):
        basis_rows[2 * wave_index] = np.sqrt(2.0 / plane_count) * np.cos(
            2.0 * np.pi * wave_index * positions / plane_count
        )
        basis_rows[2 * wave_index + 1] = np.sqrt(2.0 / plane_count) * np.sin(
            2.0 * np.pi * wave_index * positions / plane_count
        )
    wave_counts = np.arange(plane_count) // 2
    wave_counts[1] = plane_count // 2
    wave_counts[0] = 0
    wavenumbers = 2.0 * np.pi * wave_counts / (plane_count / 64.0)
    rotate = np.zeros((plane_count, plane_count))
    for wave_index in range(1, plane_count // 2):
        rotate[2 * wave_index, 2 * wave_index + 1] = wavenumbers[2 * wave_index]
        rotate[2 * wave_index + 1, 2 * wave_index] = -wavenumbers[2 * wave_index]
    return basis_rows, basis_rows.T @ rotate @ basis_rows


def two_parts(table):
    table = table.astype(np.float32)
    high = table.astype(jnp.bfloat16)
    low = (table - high.astype(np.float32)).astype(jnp.bfloat16)
    return high, low


def split_values(values):
    high = values.astype(jnp.bfloat16)
    low = (values - high.astype(jnp.float32)).astype(jnp.bfloat16)
    return high, low


def three_parts(values):
    high = values.astype(jnp.bfloat16)
    rest = values - high.astype(jnp.float32)
    middle = rest.astype(jnp.bfloat16)
    return high, middle, (rest - middle.astype(jnp.float32)).astype(jnp.bfloat16)


def dot(left, right):
    return jnp.dot(left, right, preferred_element_type=jnp.float32)


def dot_three(values, high, low):
    vh, vl = split_values(values)
    return dot(vh, high) + (dot(vl, high) + dot(vh, low))


def times(matrix, values, sign):
    n = len(values)
    half = n // 2
    even = [values[m] + values[n - 1 - m] for m in range(half)]
    odd = [values[m] - values[n - 1 - m] for m in range(half)]
    out = [None] * n
    for k in range(half + 1):
        s = None
        d = None
        for m in range(half):
            ce = 0.5 * (matrix[k, m] + matrix[k, n - 1 - m])
            co = 0.5 * (matrix[k, m] - matrix[k, n - 1 - m])
            if not (k == half and sign < 0):
                term = float(ce) * even[m]
                s = term if s is None else s + term
            if not (k == half and sign > 0):
                term = float(co) * odd[m]
                d = term if d is None else d + term
        if not (k == half and sign < 0):
            s = s + float(matrix[k, half]) * values[half]
        if k == half:
            out[k] = s if sign > 0 else d
        else:
            out[k] = s + d
            out[n - 1 - k] = s - d if sign > 0 else d - s
    return out


def swap_halves(a, b, low):
    axis = a.ndim - 2
    return (
        jnp.where(low, a, pltpu.roll(b, 4, axis)),
        jnp.where(low, pltpu.roll(a, 4, axis), b),
    )


def chunk_start(step, size, total):
    return jnp.minimum(step * size, total - size)


def section_kernel(
    sizes,
    derivative,
    weights,
    adj_ref,
    flow_ref,
    place_ref,
    wh_ref,
    wl_ref,
    vh_ref,
    vl_ref,
    dh_ref,
    dl_ref,
    widths_ref,
    heights_ref,
    phase_ref,
    wq_ref,
    final_ref,
    coef_ref,
    out_ref,
    base_rows,
    wide_rows,
    send1,
    recv1,
    send2,
    recv2,
    base_now,
    base_slope,
    lines,
    line_z,
    acc,
    res,
    image,
    direction,
    along,
    edges,
    ghosts,
    sums,
    sums_in,
    send1_sem,
    recv1_sem,
    send2_sem,
    recv2_sem,
    local_sem,
    edge_send_sem,
    edge_recv_sem,
    sum_send_sem,
    sum_recv_sem,
):
    n_four, n_elem = sizes
    q = 11
    elem = lax.axis_index("elem")
    four = lax.axis_index("four")
    stiff = derivative.T @ (weights[:, None] * derivative)

    barrier = pltpu.get_barrier_semaphore()
    for k in range(1, n_four):
        pl.semaphore_signal(
            barrier, inc=1, device_id=(elem, lax.rem(four + k, n_four)), device_id_type=MESH
        )
    for k in range(1, n_elem):
        pl.semaphore_signal(
            barrier, inc=1, device_id=(lax.rem(elem + k, n_elem), four), device_id_type=MESH
        )

    low3 = lax.broadcasted_iota(jnp.int32, (1, 8, LANES), 1) < 4
    low3w = lax.broadcasted_iota(jnp.int32, (1, 8, 256), 1) < 4

    lane8 = lax.broadcasted_iota(jnp.int32, (8, LANES), 1)

    def spread(c):
        def turn(qy, carry):
            blocks = []
            for ey in range(2):
                tiles = [adj_ref[c, qy, pl.ds(2 * w + ey, 8, stride=22), :] for w in range(11)]
                for jl in range(8):
                    w, o = (176 * jl) // LANES, (176 * jl) % LANES
                    pair = [tiles[w], tiles[w + 1], tiles[min(w + 2, 10)]]
                    if o:
                        pair = [pltpu.roll(x, LANES - o, 1) for x in pair]
                        keep = lane8 < LANES - o
                        pair = [jnp.where(keep, pair[0], pair[1]), jnp.where(keep, pair[1], pair[2])]
                    blocks.append(jnp.concatenate(pair[:2], axis=1))
            block = jnp.concatenate(blocks, axis=0)
            total = None
            for piece in three_parts(block):
                term = lax.dot_general(
                    place_ref[...],
                    piece,
                    (((1,), (1,)), ((), ())),
                    preferred_element_type=jnp.float32,
                )
                total = term if total is None else total + term
            coef_ref[c, pl.ds(qy * 11, 11)] = total.reshape(11, 16, LANES)
            return carry

        lax.fori_loop(0, 11, turn, 0)
        coef_ref[c, NODES] = jnp.zeros((16, LANES), jnp.float32)

    def gather(c, low, high):
        def turn(qy, carry):
            block = out_ref[c, pl.ds(qy * 11, 11)].reshape(176, LANES)
            block = jnp.concatenate([block, jnp.zeros((80, LANES), jnp.float32)], axis=0).T
            total = None
            for piece in three_parts(block):
                term = dot(piece[:, :176], place_ref[...])
                total = term if total is None else total + term
            for ey in range(2):
                for w in range(11):
                    done = None
                    at = 0
                    while at < LANES:
                        jl, node = divmod(LANES * w + at, 176)
                        side = 0 if node < LANES else 1
                        length = min((LANES if side == 0 else 176) - node, LANES - at)
                        row = (ey * 8 + jl) * 8
                        value = total[row : row + 8, LANES * side : LANES * (side + 1)]
                        move = (at - (node - LANES * side)) % LANES
                        if move:
                            value = pltpu.roll(value, move, 1)
                        done = value if done is None else jnp.where(lane8 < at, done, value)
                        at += length
                    final_ref[c, qy, pl.ds(2 * w + ey, 8, stride=22), :] = done
            return carry

        lax.fori_loop(low, high, turn, 0)

    pending = []

    def fill():
        if pending:
            pending.pop(0)()

    def pack(c):
        def body(step, carry):
            t = chunk_start(step, 8, TILES)
            for tile in range(2):
                a = coef_ref[c, pl.ds(t, 8), pl.ds(8 * tile, 8), :]
                b = coef_ref[c, pl.ds(t + TILES, 8), pl.ds(8 * tile, 8), :]
                first, second = swap_halves(a, b, low3)
                send1[2 * tile, c, pl.ds(t, 8)] = first
                send1[2 * tile + 1, c, pl.ds(t, 8)] = second
            return carry

        lax.fori_loop(0, 8, body, 0)

    def exchange(source, target, send_sem, recv_sem, c):
        return [
            pltpu.make_async_remote_copy(
                src_ref=source.at[lax.rem(four + k, n_four), c],
                dst_ref=target.at[four, c],
                send_sem=send_sem.at[c, k],
                recv_sem=recv_sem.at[c, k],
                device_id=(elem, lax.rem(four + k, n_four)),
                device_id_type=MESH,
            )
            for k in range(1, n_four)
        ]

    def own(source, target, c, which):
        return pltpu.make_async_copy(source.at[four, c], target.at[four, c], local_sem.at[which, c])

    copies1 = [exchange(send1, recv1, send1_sem, recv1_sem, c) for c in range(3)]
    own1 = [own(send1, recv1, c, 0) for c in range(3)]
    copies2 = [exchange(send2, recv2, send2_sem, recv2_sem, c) for c in range(3)]
    own2 = [own(send2, recv2, c, 1) for c in range(3)]

    spread(0)
    pack(0)
    pl.semaphore_wait(barrier, n_four - 1 + n_elem - 1)
    for copy in copies1[0]:
        copy.start()
    own1[0].start()
    for c in (1, 2):
        spread(c)
        pack(c)
        for copy in copies1[c]:
            copy.start()
        own1[c].start()

    row_w = lax.broadcasted_iota(jnp.int32, (8, LANES), 0)
    first_column = four * 4
    hx = jnp.zeros((8, LANES), jnp.float32)
    hy = jnp.zeros((8, LANES), jnp.float32)
    for i in range(8):
        hx = jnp.where(row_w == i, widths_ref[first_column + i % 4], hx)
        hy = jnp.where(row_w == i, heights_ref[i // 4], hy)
    gx = 2.0 / hx
    gy = 2.0 / hy

    phase = phase_ref[0]
    shift_row = lax.broadcasted_iota(jnp.int32, (256, 256), 0)
    shift_col = lax.broadcasted_iota(jnp.int32, (256, 256), 1)
    moved = jnp.where(shift_row + phase >= 256, shift_row + phase - 256, shift_row + phase)
    shift = jnp.where(moved == shift_col, 1.0, 0.0).astype(jnp.bfloat16)

    for c in range(3):

        def place_body(qy, carry, c=c):
            wide_rows[...] = flow_ref[c, qy].astype(jnp.float32)
            at = pl.multiple_of(qy * 88, 8)
            for qx in range(q):
                for h in range(2):
                    for ey in range(2):
                        rows = wide_rows[pl.ds(qx * 4 + h * 2 + ey, 4, stride=44), :]
                        base_rows[h, pl.ds(at + qx * 8 + ey * 4, 4), :] = rows
            return carry

        lax.fori_loop(0, 11, place_body, 0)

        def roll_body(step, carry, c=c):
            n = step * 11
            at = pl.ds(pl.multiple_of(n * 8, 8), 88)
            rows = jnp.concatenate([base_rows[0, at, :], base_rows[1, at, :]], axis=1)
            now = dot(rows.astype(jnp.bfloat16), shift)
            base_now[c, pl.ds(n, 11)] = now.reshape(11, 8, 256)
            now_b = now.astype(jnp.bfloat16)
            slope = dot(now_b, dh_ref[...]) + dot(now_b, dl_ref[...])
            base_slope[c, 2, pl.ds(n, 11)] = slope.reshape(11, 8, 256)
            return carry

        lax.fori_loop(0, 11, roll_body, 0)

        def slope_body(step, carry, c=c):
            for h in range(2):
                part = pl.ds(LANES * h, LANES)
                turned = times(
                    derivative, [base_now[c, step * 11 + m, :, part] for m in range(q)], -1
                )
                for k in range(q):
                    base_slope[c, 0, step * 11 + k, :, part] = gx * turned[k]
                turned = times(
                    derivative, [base_now[c, m * 11 + step, :, part] for m in range(q)], -1
                )
                for k in range(q):
                    base_slope[c, 1, k * 11 + step, :, part] = gy * turned[k]
            return carry

        lax.fori_loop(0, 11, slope_body, 0)

    for c in range(3):
        acc[c, NODES] = jnp.zeros((8, 256), jnp.float32)
    edges[...] = jnp.zeros(edges.shape, jnp.float32)
    sums[...] = jnp.zeros(sums.shape, jnp.float32)

    def send_back(c):
        def back_body(step, carry):
            t = chunk_start(step, 8, TILES)
            a = acc[c, pl.ds(t, 8)]
            b = acc[c, pl.ds(t + TILES, 8)]
            e0, e1 = swap_halves(a, b, low3w)
            e0 = e0.reshape(64, 256)
            e1 = e1.reshape(64, 256)
            out = dot_three(e0, vh_ref[pl.ds(0, 256), :], vl_ref[pl.ds(0, 256), :])
            out = out + dot_three(e1, vh_ref[pl.ds(256, 256), :], vl_ref[pl.ds(256, 256), :])
            for s in range(n_four):
                send2[s, c, pl.ds(t, 8)] = out[:, LANES * s : LANES * (s + 1)].reshape(8, 8, LANES)
            return carry

        lax.fori_loop(0, 8, back_body, 0)
        for copy in copies2[c]:
            copy.start()
        own2[c].start()

    for c in range(3):
        for copy in copies1[c]:
            copy.wait_recv()
        own1[c].wait()

        def line_body(step, carry, c=c):
            t = chunk_start(step, 8, TILES)
            out = None
            for s in range(n_four):
                rows = recv1[s, c, pl.ds(t, 8)].reshape(64, LANES)
                part = dot_three(
                    rows, wh_ref[pl.ds(s * LANES, LANES), :], wl_ref[pl.ds(s * LANES, LANES), :]
                )
                out = part if out is None else out + part
            e0 = out[:, :256].reshape(8, 8, 256)
            e1 = out[:, 256:].reshape(8, 8, 256)
            a, b = swap_halves(e0, e1, low3w)
            lines[pl.ds(t, 8)] = a
            lines[pl.ds(t + TILES, 8)] = b
            return carry

        lax.fori_loop(0, 8, line_body, 0)

        def take_body(step, carry, c=c):
            for k in range(q):
                n = step * 11 + k
                value = lines[n]
                for e in range(3):
                    if e != c:
                        change = -value * base_slope[c, e, n]
                        acc[e, n] = change if c == 0 else acc[e, n] + change
            return carry

        lax.fori_loop(0, 11, take_body, 0)
        if c == 2:
            send_back(0)
            send_back(1)

        def span_body(step, carry):
            n = step * 11
            rows = lines[pl.ds(n, 11)].reshape(88, 256)
            line_z[pl.ds(n, 11)] = dot_three(rows, dh_ref[...], dl_ref[...]).reshape(11, 8, 256)
            return carry

        lax.fori_loop(0, 11, span_body, 0)

        def add_x(step, carry, c=c):
            for h in range(2):
                part = pl.ds(LANES * h, LANES)
                values = [lines[step * 11 + m, :, part] for m in range(q)]
                turned = times(derivative, values, -1)
                for k in range(q):
                    n = step * 11 + k
                    gain = base_now[0, n, :, part] * (gx * turned[k])
                    gain = gain + base_now[2, n, :, part] * line_z[n, :, part]
                    gain = gain - values[k] * base_slope[c, c, n, :, part]
                    if c > 0:
                        gain = gain + acc[c, n, :, part]
                    acc[c, n, :, part] = gain
            return carry

        lax.fori_loop(0, 11, add_x, 0)

        def add_y(step, carry, c=c):
            for h in range(2):
                part = pl.ds(LANES * h, LANES)
                values = [lines[m * 11 + step, :, part] for m in range(q)]
                turned = times(derivative, values, -1)
                for k in range(q):
                    n = k * 11 + step
                    acc[c, n, :, part] += base_now[1, n, :, part] * (gy * turned[k])
            return carry

        lax.fori_loop(0, 11, add_y, 0)
        if c == 2:
            send_back(2)

    lane = lax.broadcasted_iota(jnp.int32, (8, LANES), 1)
    row = lax.broadcasted_iota(jnp.int32, (8, LANES), 0)
    lower = lane < 64
    lane_half = jnp.where(lower, lane, lane - 64)
    lane_plane = lax.rem(lane_half, 8) * 8 + lane_half // 8 + four * 64
    kappa = lane_plane // 2
    kappa = jnp.where(lane_plane == 1, 32 * n_four, kappa)
    kappa = jnp.where(lane_plane == 0, 0, kappa)
    beta = kappa.astype(jnp.float32) * np.float32(2.0 * np.pi / n_four)
    wave = beta * beta + SIGMA
    hyl = jnp.where(lower, heights_ref[0], heights_ref[1])
    hxl = []
    for tile in range(2):
        h = jnp.zeros((8, LANES), jnp.float32)
        for i in range(8):
            h = jnp.where(row == i, widths_ref[8 * tile + i], h)
        hxl.append(h)
    quarter = [0.25 * h * hyl for h in hxl]
    scale_x = [hyl / h for h in hxl]
    scale_y = [h / hyl for h in hxl]
    one = jnp.ones((8, LANES), jnp.float32)
    half = 0.5 * one
    left_inner = elem > 0
    right_inner = elem < n_elem - 1
    share_first = [jnp.where(jnp.logical_and(row == 0, jnp.logical_not(left_inner)), one, half), half]
    share_last = [half, jnp.where(jnp.logical_and(row == 7, jnp.logical_not(right_inner)), one, half)]
    share_top = jnp.where(lower, one, half)
    share_bottom = jnp.where(lower, half, one)
    right = lax.rem(elem + 1, n_elem)
    left = lax.rem(elem + n_elem - 1, n_elem)

    def edge_copies(c, level):
        return [
            pltpu.make_async_remote_copy(
                src_ref=edges.at[c, level, 0],
                dst_ref=ghosts.at[c, level, 1],
                send_sem=edge_send_sem.at[c, level, 0],
                recv_sem=edge_recv_sem.at[c, level, 1],
                device_id=(left, four),
                device_id_type=MESH,
            ),
            pltpu.make_async_remote_copy(
                src_ref=edges.at[c, level, 1],
                dst_ref=ghosts.at[c, level, 0],
                send_sem=edge_send_sem.at[c, level, 1],
                recv_sem=edge_recv_sem.at[c, level, 0],
                device_id=(right, four),
                device_id_type=MESH,
            ),
        ]

    def edge_start(values, c, level):
        for qy in range(q):
            edges[c, level, 0, pl.ds(qy, 1), :] = values[qy * 11, pl.ds(0, 1), :]
            edges[c, level, 1, pl.ds(qy, 1), :] = values[qy * 11 + 10, pl.ds(15, 1), :]
        copies = edge_copies(c, level)
        for copy in copies:
            copy.start()
        return copies

    left_keep = jnp.where(left_inner, 1.0, 0.0)
    right_keep = jnp.where(right_inner, 1.0, 0.0)

    def assemble_here(values, c, level, copies):
        fill()
        for copy in copies:
            copy.wait_recv()

        def body(qy, carry):
            n0 = qy * 11
            a0 = values[n0, pl.ds(0, 8), :]
            a1 = values[n0, pl.ds(8, 8), :]
            b0 = values[n0 + 10, pl.ds(0, 8), :]
            b1 = values[n0 + 10, pl.ds(8, 8), :]
            from_left = ghosts[c, level, 0, pl.ds(qy, 1), :] * left_keep
            from_right = ghosts[c, level, 1, pl.ds(qy, 1), :] * right_keep
            rb0 = pltpu.roll(b0, 1, 0)
            rb1 = pltpu.roll(b1, 1, 0)
            ra0 = pltpu.roll(a0, 7, 0)
            ra1 = pltpu.roll(a1, 7, 0)
            values[n0, pl.ds(0, 8), :] = a0 + jnp.where(row == 0, from_left, rb0)
            values[n0, pl.ds(8, 8), :] = a1 + jnp.where(row == 0, rb0, rb1)
            values[n0 + 10, pl.ds(0, 8), :] = b0 + jnp.where(row == 7, ra1, ra0)
            values[n0 + 10, pl.ds(8, 8), :] = b1 + jnp.where(row == 7, from_right, ra1)
            return carry

        lax.fori_loop(0, q, body, 0)
        for qx in range(q):
            for tile in range(2):
                rows = pl.ds(8 * tile, 8)
                top = values[qx, rows, :]
                bottom = values[110 + qx, rows, :]
                values[qx, rows, :] = top + jnp.where(lower, 0.0, pltpu.roll(bottom, 64, 1))
                values[110 + qx, rows, :] = bottom + jnp.where(lower, pltpu.roll(top, 64, 1), 0.0)

    def sum_copies(c, level):
        return [
            pltpu.make_async_remote_copy(
                src_ref=sums.at[c, level],
                dst_ref=sums_in.at[c, level, k],
                send_sem=sum_send_sem.at[c, level, k],
                recv_sem=sum_recv_sem.at[c, level, k],
                device_id=(lax.rem(elem + k, n_elem), four),
                device_id_type=MESH,
            )
            for k in range(1, n_elem)
        ]

    zero = jnp.zeros((8, LANES), jnp.float32)

    def apply(values, target):
        def body_x(qy, carry):
            rr, wy = carry[0], wq_ref[qy]
            share = jnp.where(qy == 0, share_top, jnp.where(qy == q - 1, share_bottom, one))
            for tile in range(2):
                rows = pl.ds(8 * tile, 8)
                v = [values[qy * 11 + m, rows, :] for m in range(q)]
                turned = times(stiff, v, 1)
                ax = scale_x[tile] * wy
                mass = (wave * quarter[tile]) * wy
                inner = None
                for k in range(q):
                    target[qy * 11 + k, rows, :] = ax * turned[k] + (mass * float(weights[k])) * v[k]
                    square = v[k] * v[k]
                    if k == 0:
                        square = square * share_first[tile]
                    if k == q - 1:
                        square = square * share_last[tile]
                    inner = square if inner is None else inner + square
                rr = rr + share * inner
            return (rr,)

        (rr,) = lax.fori_loop(0, q, body_x, (zero,))

        def body_y(qx, carry):
            product, wx = carry[0], wq_ref[qx]
            for tile in range(2):
                rows = pl.ds(8 * tile, 8)
                v = [values[m * 11 + qx, rows, :] for m in range(q)]
                turned = times(stiff, v, 1)
                ay = scale_y[tile] * wx
                for k in range(q):
                    total = target[k * 11 + qx, rows, :] + ay * turned[k]
                    target[k * 11 + qx, rows, :] = total
                    product = product + v[k] * total
            return (product,)

        (product,) = lax.fori_loop(0, q, body_y, (zero,))
        return rr, product

    def fold(values):
        total = jnp.sum(values, axis=0, keepdims=True)
        return total + pltpu.roll(total, 64, 1)

    waiting = []
    for c in range(3):
        for copy in copies2[c]:
            copy.wait_recv()
        own2[c].wait()

        def unpack_body(step, carry, c=c):
            t = chunk_start(step, 8, TILES)
            for tile in range(2):
                rows = pl.ds(8 * tile, 8)
                a, b = swap_halves(
                    recv2[2 * tile, c, pl.ds(t, 8)], recv2[2 * tile + 1, c, pl.ds(t, 8)], low3
                )
                res[pl.ds(t, 8), rows, :] = SIGMA * coef_ref[c, pl.ds(t, 8), rows, :] + a / NU
                res[pl.ds(t + TILES, 8), rows, :] = (
                    SIGMA * coef_ref[c, pl.ds(t + TILES, 8), rows, :] + b / NU
                )
            return carry

        lax.fori_loop(0, 8, unpack_body, 0)

        def mass_body(qy, carry):
            wy = wq_ref[qy]
            for tile in range(2):
                rows = pl.ds(8 * tile, 8)
                area = quarter[tile] * wy
                for k in range(q):
                    res[qy * 11 + k, rows, :] = res[qy * 11 + k, rows, :] * (area * float(weights[k]))
            return carry

        lax.fori_loop(0, q, mass_body, 0)
        copies = edge_start(res, c, 0)
        waiting += copies
        assemble_here(res, c, 0, copies)

        norm_now = None
        step_size = None
        for it in range(ITERS):
            rr, product = apply(res, image)
            sums[c, it, pl.ds(0, 1), :] = fold(rr)
            sums[c, it, pl.ds(1, 1), :] = fold(product)
            sum_list = sum_copies(c, it)
            for copy in sum_list:
                copy.start()
            waiting += sum_list
            if it + 1 < ITERS:
                copies = edge_start(image, c, it + 1)
                waiting += copies
                assemble_here(image, c, it + 1, copies)
            else:
                fill()
            for copy in sum_list:
                copy.wait_recv()
            total = sums[c, it]
            for k in range(1, n_elem):
                total = total + sums_in[c, it, k]
            norm_next = total[0:1, :]
            product = total[1:2, :]
            if it == 0:
                growth = jnp.zeros_like(norm_next)
                step_size = norm_next / product
            else:
                growth = norm_next / norm_now
                step_size = norm_next / (product - growth * norm_next / step_size)
            norm_now = norm_next

            def update(n, carry, it=it, c=c, growth=growth, step_size=step_size):
                for j in range(11):
                    m = n * 11 + j
                    r = res[m]
                    if it == 0:
                        d = r
                        out_ref[c, m] = step_size * d
                    else:
                        d = r + growth * direction[m]
                        out_ref[c, m] = out_ref[c, m] + step_size * d
                    if it + 1 < ITERS:
                        direction[m] = d
                        a = image[m]
                        if it > 0:
                            a = a + growth * along[m]
                        if it + 2 < ITERS:
                            along[m] = a
                        res[m] = r - step_size * a
                return carry

            lax.fori_loop(0, 11, update, 0)
        pending += [functools.partial(gather, c, i, min(i + 4, 11)) for i in (0, 4, 8)]

    while pending:
        fill()

    for group in copies1 + copies2 + [waiting]:
        for copy in group:
            copy.wait_send()


def fold_rows(values):
    values = values.reshape(3, 2, 11, 88, LANES)
    return jnp.transpose(values, (0, 2, 3, 1, 4)).reshape(3, 11, 176, LANES)


def local_blocks(adjoint_velocity, base_flow, column_widths, row_heights, base_phase):
    n_four, n_elem = lax.axis_size("four"), lax.axis_size("elem")
    derivative, weights = gll_numbers(11)
    basis_rows, span_slope = span_numbers(256)
    forward = np.zeros((n_four, 2, 64, 2, 256))
    order = np.arange(64).reshape(8, 8).T.reshape(64)
    for ey in range(2):
        forward[:, ey, :, ey, :] = basis_rows.reshape(n_four, 64, 256)[:, order]
    forward = forward.reshape(512, 512)
    tables = two_parts(forward) + two_parts(forward.T) + two_parts(span_slope.T)
    place = np.zeros((11, 16, 256), np.float32)
    for column in range(16):
        for qx in range(11):
            place[qx, column, column * 11 + qx] = 1.0
    place = place.reshape(176, 256).astype(jnp.bfloat16)
    vmem = pl.BlockSpec(memory_space=pltpu.VMEM)
    smem = pl.BlockSpec(memory_space=pltpu.SMEM)
    f32 = jnp.float32
    blocks = (n_four, 3, TILES, 8, LANES)
    field = (PAD, 16, LANES)
    dma = pltpu.SemaphoreType.DMA
    out = pl.pallas_call(
        lambda *refs: section_kernel((n_four, n_elem), derivative, weights, *refs),
        out_shape=jax.ShapeDtypeStruct((3, 11, 176, LANES), f32),
        in_specs=[vmem] * 9 + [smem] * 4,
        out_specs=vmem,
        scratch_shapes=[
            pltpu.VMEM((3, PAD, 16, LANES), f32),
            pltpu.VMEM((3, NODES, 16, LANES), f32),
            pltpu.VMEM((2, NODES * 8, LANES), f32),
            pltpu.VMEM((176, LANES), f32),
            pltpu.VMEM(blocks, f32),
            pltpu.VMEM(blocks, f32),
            pltpu.VMEM(blocks, f32),
            pltpu.VMEM(blocks, f32),
            pltpu.VMEM((3, NODES, 8, 256), f32),
            pltpu.VMEM((3, 3, NODES, 8, 256), f32),
            pltpu.VMEM((PAD, 8, 256), f32),
            pltpu.VMEM((PAD, 8, 256), f32),
            pltpu.VMEM((3, PAD, 8, 256), f32),
            pltpu.VMEM(field, f32),
            pltpu.VMEM(field, f32),
            pltpu.VMEM(field, f32),
            pltpu.VMEM(field, f32),
            pltpu.VMEM((3, ITERS, 2, 16, LANES), f32),
            pltpu.VMEM((3, ITERS, 2, 16, LANES), f32),
            pltpu.VMEM((3, ITERS, 8, LANES), f32),
            pltpu.VMEM((3, ITERS, n_elem, 8, LANES), f32),
            dma((3, n_four)),
            dma((3, n_four)),
            dma((3, n_four)),
            dma((3, n_four)),
            dma((2, 3)),
            dma((3, ITERS, 2)),
            dma((3, ITERS, 2)),
            dma((3, ITERS, n_elem)),
            dma((3, ITERS, n_elem)),
        ],
        compiler_params=pltpu.CompilerParams(
            collective_id=0, has_side_effects=True, vmem_limit_bytes=60 * 1024 * 1024
        ),
    )(fold_rows(adjoint_velocity), fold_rows(base_flow), place, *tables, column_widths, row_heights, base_phase, weights.astype(np.float32))
    out = jnp.transpose(out.reshape(3, 11, 88, 2, LANES), (0, 3, 1, 2, 4))
    return out.reshape(adjoint_velocity.shape)


def local(adjoint_velocity, base_flow, column_widths, row_heights, base_phase):
    four, elem = lax.axis_size("four"), lax.axis_size("elem")
    known = (
        adjoint_velocity.shape == (3, 2, 11, 64 * 16 * 11)
        and column_widths.shape == (16,)
        and four == 4
        and elem > 2
    )
    chosen = local_blocks if known else local_general
    return chosen(adjoint_velocity, base_flow, column_widths, row_heights, base_phase)


def solution(mesh):
    return jax.shard_map(
        local,
        mesh=mesh,
        in_specs=(
            P(None, None, None, ("elem", "four")),
            P(None, None, None, ("elem", "four")),
            P("elem"),
            P(),
            P(),
        ),
        out_specs=P(None, None, None, ("elem", "four")),
        check_vma=False,
    )
```
